32 devices in a mesh: dp: 8 (over z, core), seq: 4 (over y, x).
Axes of the slice: x: 2, y: 2, z: 4, core: 2. Of those that a mesh axis runs over, the one named last changes fastest.
Arguments:
- mixer_in: bfloat16 [8192, 2816], P(('dp', 'seq')), parts along dimension 0, may hold values from -92 to 92
- gate_input: bfloat16 [8192, 2560], P(('dp', 'seq')), parts along dimension 0, may hold values from -6 to 6
- step_raw: bfloat16 [8192, 40], P(('dp', 'seq')), parts along dimension 0, may hold values from -6 to 6
- lengths: int32 [24], P('dp'), parts along dimension 0, may hold values from 1 to 512, 1024 in all
- deal_order: int32 [32], P('dp'), parts along dimension 0, may hold values from 0 to 3, as said below
- conv_weight: float32 [4, 2816], replicated, may hold values from -3 to 3
- conv_bias: float32 [2816], replicated, may hold values from -3 to 3
- step_bias: float32 [40], replicated, may hold values from -4 to -1
- decay_rate: float32 [40], replicated, may hold values from 0.01 to 2
- skip_gain: float32 [40], replicated, may hold values from 0.5 to 1.5
- norm_gain: float32 [2560], replicated, may hold values from 0.5 to 1.5
Outputs:
- mixed_out: bfloat16 [8192, 2560], P(('dp', 'seq')), parts along dimension 0
- final_states: float32 [24, 2560, 128], P('dp', 'seq'), parts along dimension 0
The draws below stay inside these ranges and needn't reach their ends.
There are 8 independent parts, one for each index of `dp`. The reference program is written for one: setup_inputs(seed, part) draws one part's arguments, and reference() takes and returns one part's arrays. A program takes and returns all parts, laid end to end along the dimension named above; an argument that names none is the same for every part. Nothing has to cross between parts.
Inputs may be any that keep to these rules, and one draw needn't show every extreme that they name: The prompt lengths sum to 1024 and the longest is exactly 512. `deal_order`: every sequence stretch stands in exactly one dealt slot.
All inputs are finite; a program needn't handle non-finite values.
Results may differ from the reference program's by a relative error of at most 0.005.
Values may be sent and summed in bfloat16 or wider, within the bound.
A program may use at most 128 MiB of HBM per device.

```python
import math
import jax
import jax.numpy as jnp
import numpy as np
from jax import lax

HEADS = 40
HEAD_DIM = 64
STATE = 128
KERNEL = 4
STRETCH = 256
DOCS = 3
INNER = 2560
CHANNELS = 2816
STREAM = 1024
STRETCHES = 4
LONGEST = 512


def dealt_slots(key):
    return jax.random.permutation(jax.random.fold_in(key, 31), STRETCHES).astype(jnp.int32)


def draw_deal_order(key, part):
    return dealt_slots(key)


def draw_mixer_in(key, part):
    sign_key = jax.random.fold_in(key, 41)
    noise_key = jax.random.fold_in(key, 43)
    loud_key = jax.random.fold_in(key, 47)
    pattern = 0.6 * jax.random.rademacher(sign_key, (CHANNELS,), dtype=jnp.float32)
    noise = jnp.clip(jax.random.normal(noise_key, (STREAM, CHANNELS), jnp.float32), -4.0, 4.0)
    loud = jnp.exp(jax.random.uniform(loud_key, (STRETCHES, HEADS), jnp.float32, 0.0, math.log(20.0)))
    columns = jnp.concatenate([jnp.repeat(loud, HEAD_DIM, axis=1), jnp.ones((STRETCHES, 2 * STATE), jnp.float32)], 1)
    row_scale = jnp.repeat(columns, STRETCH, axis=0)
    return (row_scale * (pattern[None, :] + noise)).astype(jnp.bfloat16)


def level_of(own_key, shape, pieces, smallest, high):
    def one(position, blocks):
        heights = jax.random.uniform(jax.random.fold_in(jax.random.fold_in(own_key, 6), position), (blocks,), jnp.float32, smallest / len(pieces), high / len(pieces))
        return jnp.repeat(jnp.exp(heights), shape[position] // blocks).reshape((-1,) + (1,) * (len(shape) - position - 1))

    level = one(*pieces[0])
    for cut in pieces[1:]:
        level = level * one(*cut)
    return level


def split_up(amount, total, most, slope):
    weights = [(1 << 20) // math.isqrt(rank ** slope) + 1 for rank in range(2, amount + 1)]
    surplus, counts = total - most - (amount - 1), [1] * (amount - 1)
    while surplus > 0:
        candidates = [i for i in range(amount - 1) if counts[i] < most]
        pool, remaining = sum([weights[i] for i in candidates]), surplus
        for i in candidates:
            addition = min(most - counts[i], max(1, remaining * weights[i] // pool), surplus)
            counts[i] = counts[i] + addition
            surplus = surplus - addition
    return np.array([most] + counts)


def uneven(own_key, number_of, total, most, skew):
    if number_of == 2:
        one = jax.random.randint(own_key, (), max(1, total - most), min(most, total - 1) + 1)
        return jnp.stack([one, total - one])
    tallies = jnp.asarray(split_up(number_of, total, most, skew), jnp.int32)
    couples = (number_of - 1) // 2
    giver, receiver = tallies[1:1 + 2 * couples:2], tallies[2:2 + 2 * couples:2]
    room = jnp.minimum(giver - 1, most - receiver)
    passed = jax.random.randint(jax.random.fold_in(own_key, 1), (couples,), 0, 1 << 20) % (room + 1)
    tallies = tallies.at[1:1 + 2 * couples:2].set(giver - passed).at[2:2 + 2 * couples:2].set(receiver + passed)
    return tallies[jax.random.permutation(jax.random.fold_in(own_key, 2), number_of)]


def scatter_about(own_key, dims, deviation, bound, shards=(), held_as=jnp.bfloat16):
    result = jax.random.normal(own_key, dims, jnp.float32) * deviation
    if len(shards) > 0:
        result = level_of(own_key, dims, shards, -0.22, 0.18) * result
    return jnp.clip(result, min=-bound, max=bound).astype(held_as)


def setup_inputs(seed: int = 0, part: int = 0) -> dict:
    streams_of = jax.random.split(jax.random.key(seed), 12)
    part_splits = jax.random.split(jax.random.fold_in(streams_of[11], part), 12)
    mixer_in = draw_mixer_in(jax.random.fold_in(jax.random.fold_in(streams_of[11], part), 71), part)
    gate_input = scatter_about(part_splits[1], (STREAM, INNER), 1.0, 6.0, ((0, 4),))
    step_raw = scatter_about(part_splits[2], (STREAM, HEADS), 1.0, 6.0, ((0, 4),))
    lengths = uneven(part_splits[3], DOCS, STREAM, LONGEST, 2).astype(jnp.int32)
    deal_order = draw_deal_order(jax.random.fold_in(jax.random.fold_in(streams_of[11], part), 71), part)
    conv_weight = scatter_about(streams_of[5], (KERNEL, CHANNELS), KERNEL ** -0.5, 3.0, (), jnp.float32)
    conv_bias = scatter_about(streams_of[6], (CHANNELS,), 0.5, 3.0, (), jnp.float32)
    step_bias = jnp.clip(jax.random.uniform(streams_of[7], (HEADS,), jnp.float32, -4.0, -1.0), -4.0, -1.0)
    decay_rate = jnp.clip(jnp.exp(jax.random.uniform(streams_of[8], (HEADS,), jnp.float32, math.log(0.01), math.log(2.0))), 0.01, 2.0)
    skip_gain = jnp.clip(jax.random.uniform(streams_of[9], (HEADS,), jnp.float32, 0.5, 1.5), 0.5, 1.5)
    norm_gain = jnp.clip(1.0 + 0.1 * jax.random.normal(streams_of[10], (INNER,), jnp.float32), 0.5, 1.5)
    return dict(mixer_in=mixer_in, gate_input=gate_input, step_raw=step_raw, lengths=lengths, deal_order=deal_order, conv_weight=conv_weight, conv_bias=conv_bias, step_bias=step_bias, decay_rate=decay_rate, skip_gain=skip_gain, norm_gain=norm_gain)


def doc_index(ends, positions):
    return lax.optimization_barrier(jnp.sum((ends[None, :] <= positions[:, None]).astype(jnp.int32), axis=1)).astype(jnp.int32)

def reference(mixer_in, gate_input, step_raw, lengths, deal_order, conv_weight, conv_bias, step_bias, decay_rate, skip_gain, norm_gain):
    inner = HEADS * HEAD_DIM

    def undeal(source):
        blocks = source.reshape((STRETCHES, STRETCH) + source.shape[1:])
        return jnp.zeros_like(blocks).at[deal_order].set(blocks).reshape(source.shape)
    packed_in = undeal(mixer_in)
    packed_gate = undeal(gate_input)
    packed_step = undeal(step_raw)
    positions = jnp.arange(STREAM, dtype=jnp.int32)
    ends = jnp.cumsum(lengths).astype(jnp.int32)
    doc_ids = doc_index(ends, positions)
    padded = jnp.concatenate([jnp.zeros((KERNEL - 1, CHANNELS), jnp.bfloat16), packed_in], 0)
    padded_doc = jnp.concatenate([jnp.full((KERNEL - 1,), -1, jnp.int32), doc_ids], 0)
    accum = jnp.zeros((STREAM, CHANNELS), jnp.float32) + conv_bias
    for offset in range(KERNEL):
        keep = (padded_doc[offset:offset + STREAM] == doc_ids).astype(jnp.float32)
        accum = accum + conv_weight[offset] * padded[offset:offset + STREAM].astype(jnp.float32) * keep[:, None]
    mixed = jax.nn.silu(accum).astype(jnp.bfloat16)
    values = mixed[:, :inner]
    input_map = mixed[:, inner:inner + STATE]
    output_map = mixed[:, inner + STATE:]
    step = jax.nn.softplus(packed_step.astype(jnp.float32) + step_bias)
    log_decay = -decay_rate * step
    running = jnp.cumsum(log_decay, axis=0)
    scaled = (values.astype(jnp.float32) * jnp.repeat(step, HEAD_DIM, axis=1)).astype(jnp.bfloat16)
    stretch_ids = jnp.arange(STRETCHES, dtype=jnp.int32)
    starts = stretch_ids * STRETCH
    base = running[starts] - log_decay[starts]
    stretch_end = running[starts + STRETCH - 1]
    end_doc = doc_ids[starts + STRETCH - 1]
    prev_doc = jnp.where(stretch_ids > 0, doc_ids[jnp.maximum(starts - 1, 0)], -1).astype(jnp.int32)

    def blocked(source):
        return source.reshape((STRETCHES, STRETCH) + source.shape[1:])

    def local_state(inputs):
        scaled_c, keys_c, running_c, doc_c = inputs
        weight = jnp.exp(jnp.where((doc_c == doc_c[-1])[:, None], running_c[-1][None, :] - running_c, -jnp.inf))
        weighted = (scaled_c.astype(jnp.float32) * jnp.repeat(weight, HEAD_DIM, axis=1)).astype(jnp.bfloat16)
        return jnp.dot(weighted.T, keys_c, preferred_element_type=jnp.float32)
    states = lax.map(local_state, (blocked(scaled), blocked(input_map), blocked(running), blocked(doc_ids)))
    allowed = (stretch_ids[None, :] < stretch_ids[:, None]) & (end_doc[None, :] == prev_doc[:, None])
    gaps = jnp.exp(jnp.where(allowed[:, :, None], base[:, None, :] - stretch_end[None, :, :], -jnp.inf))

    def inflow(gap_row):
        return jnp.einsum('ck,ckn->kn', jnp.repeat(gap_row, HEAD_DIM, axis=1), states, precision=lax.Precision.HIGHEST)
    state_in = lax.map(inflow, gaps)
    lane = jnp.arange(STRETCH, dtype=jnp.int32)
    later = lane[:, None] >= lane[None, :]

    def stretch_out(inputs):
        values_c, scaled_c, keys_c, queries_c, running_c, doc_c, base_c, prev_c, state_c = inputs
        scores = jnp.dot(queries_c, keys_c.T, preferred_element_type=jnp.float32)
        same = (doc_c[:, None] == doc_c[None, :]) & later
        spans = running_c.T[:, :, None] - running_c.T[:, None, :]
        decay_mat = jnp.exp(jnp.where(same[None], spans, -jnp.inf))
        mixing = (scores[None] * decay_mat).astype(jnp.bfloat16)
        within = jnp.einsum('hts,shp->thp', mixing.astype(jnp.float32), scaled_c.reshape(STRETCH, HEADS, HEAD_DIM).astype(jnp.float32)).reshape(STRETCH, inner)
        readout = jnp.dot(queries_c, state_c.astype(jnp.bfloat16).T, preferred_element_type=jnp.float32)
        carry_weight = jnp.exp(jnp.where((doc_c == prev_c)[:, None], running_c - base_c[None, :], -jnp.inf))
        direct = values_c.astype(jnp.float32) * jnp.repeat(skip_gain, HEAD_DIM)[None, :]
        return within + readout * jnp.repeat(carry_weight, HEAD_DIM, axis=1) + direct
    outputs = lax.map(stretch_out, (blocked(values), blocked(scaled), blocked(input_map), blocked(output_map), blocked(running), blocked(doc_ids), base, prev_doc, state_in)).reshape(STREAM, inner)
    gated = outputs * jax.nn.silu(packed_gate.astype(jnp.float32))
    normed = gated * lax.rsqrt(lax.optimization_barrier(jnp.mean(gated * gated, axis=1, keepdims=True)) + 1e-05) * norm_gain
    mixed_out = normed.astype(jnp.bfloat16).reshape(STRETCHES, STRETCH, inner)[deal_order].reshape(STREAM, inner)

    def one_doc(document):
        last = (lax.dynamic_index_in_dim(ends, document, keepdims=False) - 1).astype(jnp.int32)
        owner = (last // STRETCH).astype(jnp.int32)
        begin = (owner * STRETCH).astype(jnp.int32)
        running_c = lax.dynamic_slice_in_dim(running, begin, STRETCH)
        doc_c = lax.dynamic_slice_in_dim(doc_ids, begin, STRETCH)
        scaled_c = lax.dynamic_slice_in_dim(scaled, begin, STRETCH)
        keys_c = lax.dynamic_slice_in_dim(input_map, begin, STRETCH)
        running_e = lax.dynamic_index_in_dim(running, last, keepdims=False)
        weight = jnp.exp(jnp.where((doc_c == document)[:, None], running_e[None, :] - running_c, -jnp.inf))
        weighted = (scaled_c.astype(jnp.float32) * jnp.repeat(weight, HEAD_DIM, axis=1)).astype(jnp.bfloat16)
        part = jnp.dot(weighted.T, keys_c, preferred_element_type=jnp.float32)
        base_c = lax.dynamic_index_in_dim(base, owner, keepdims=False)
        prev_c = lax.dynamic_index_in_dim(prev_doc, owner, keepdims=False)
        state_c = lax.dynamic_index_in_dim(state_in, owner, keepdims=False)
        carry_weight = jnp.exp(jnp.where(prev_c == document, running_e - base_c, -jnp.inf))
        return part + jnp.repeat(carry_weight, HEAD_DIM)[:, None] * state_c
    final_states = lax.map(one_doc, jnp.arange(DOCS, dtype=jnp.int32))
    return (mixed_out, final_states)
```

```python
import jax
import jax.numpy as jnp
from jax import lax
from jax.experimental import pallas as pl
from jax.experimental.pallas import tpu as pltpu
from jax.sharding import PartitionSpec as P

HEADS = 40
HEAD_DIM = 64
STATE = 128
KERNEL = 4
STRETCH = 256
DOCS = 3
INNER = 2560
CHANNELS = 2816


def doc_index(ends, positions):
    return jnp.sum((ends[None, :] <= positions[:, None]).astype(jnp.int32), axis=1)


def lower_ones(size):
    index = jnp.arange(size, dtype=jnp.int32)
    return (index[:, None] >= index[None, :]).astype(jnp.float32)


def ends_of(lengths):
    index = jnp.arange(lengths.shape[0], dtype=jnp.int32)
    return jnp.sum(jnp.where(index[:, None] >= index[None, :], lengths[None, :], 0), axis=1)


def body(
    mixer_in,
    gate_input,
    step_raw,
    lengths,
    deal_order,
    conv_weight,
    conv_bias,
    step_bias,
    decay_rate,
    skip_gain,
    norm_gain,
):
    myself = lax.axis_index("seq")
    local_rows = mixer_in.shape[0]
    stretches_here = local_rows // STRETCH
    stretch_total = deal_order.shape[0]
    ends = ends_of(lengths)
    all_stretches = jnp.arange(stretch_total, dtype=jnp.int32)
    my_stretches = lax.dynamic_slice_in_dim(deal_order, myself * stretches_here, stretches_here)
    lane = jnp.arange(STRETCH, dtype=jnp.int32)
    own_doc = doc_index(
        ends, (my_stretches[:, None] * STRETCH + lane[None, :]).reshape(-1)
    ).reshape(stretches_here, STRETCH)
    prev_own = jnp.where(my_stretches > 0, doc_index(ends, my_stretches * STRETCH - 1), -1)
    blocks_in = mixer_in.reshape(stretches_here, STRETCH, CHANNELS)
    tails = blocks_in[:, STRETCH - (KERNEL - 1) :, :]
    step_blocks = step_raw.reshape(stretches_here, STRETCH, HEADS)
    step = jax.nn.softplus(step_blocks.astype(jnp.float32) + step_bias)
    log_decay = -decay_rate * step
    all_tails, all_steps = (
        lax.all_gather(tails, "seq", axis=0, tiled=True),
        lax.all_gather(step_blocks, "seq", axis=0, tiled=True),
    )
    totals = jnp.sum(
        -decay_rate * jax.nn.softplus(all_steps.astype(jnp.float32) + step_bias), axis=1
    )
    slot_map = (deal_order[:, None] == all_stretches[None, :]).astype(jnp.float32)
    packed_totals = jnp.dot(slot_map.T, totals, precision=lax.Precision.HIGHEST)
    prefix = jnp.dot(lower_ones(stretch_total), packed_totals, precision=lax.Precision.HIGHEST)
    base = jnp.concatenate([jnp.zeros((1, HEADS), jnp.float32), prefix[:-1]], 0)
    pick_own = (my_stretches[:, None] == all_stretches[None, :]).astype(jnp.float32)
    base_own = jnp.dot(pick_own, base, precision=lax.Precision.HIGHEST)
    running = base_own[:, None, :] + jnp.einsum(
        "ts,ish->ith", lower_ones(STRETCH), log_decay, precision=lax.Precision.HIGHEST
    )
    prev_pick = (deal_order[None, :] == my_stretches[:, None] - 1).astype(jnp.bfloat16)
    prev_rows = jnp.einsum(
        "is,skc->ikc", prev_pick, all_tails, preferred_element_type=jnp.float32
    ).astype(jnp.bfloat16)
    extended = jnp.concatenate([prev_rows, blocks_in], 1)
    lead = (
        my_stretches[:, None] * STRETCH
        - (KERNEL - 1)
        + jnp.arange(KERNEL - 1, dtype=jnp.int32)[None, :]
    ).reshape(-1)
    ext_doc = jnp.concatenate(
        [doc_index(ends, lead).reshape(stretches_here, KERNEL - 1), own_doc], 1
    )
    accum = jnp.zeros((stretches_here, STRETCH, CHANNELS), jnp.float32) + conv_bias
    for offset in range(KERNEL):
        keep = (ext_doc[:, offset : offset + STRETCH] == own_doc).astype(jnp.float32)
        accum = (
            accum
            + conv_weight[offset]
            * extended[:, offset : offset + STRETCH, :].astype(jnp.float32)
            * keep[..., None]
        )
    mixed = jax.nn.silu(accum).astype(jnp.bfloat16)
    values = mixed[..., :INNER]
    input_map = mixed[..., INNER : INNER + STATE]
    output_map = mixed[..., INNER + STATE :]
    scaled = (values.astype(jnp.float32) * jnp.repeat(step, HEAD_DIM, axis=2)).astype(jnp.bfloat16)
    end_weight = jnp.exp(
        jnp.where((own_doc == own_doc[:, -1:])[..., None], running[:, -1:, :] - running, -jnp.inf)
    )
    weighted = (scaled.astype(jnp.float32) * jnp.repeat(end_weight, HEAD_DIM, axis=2)).astype(
        jnp.bfloat16
    )
    states = jnp.einsum("isk,isn->ikn", weighted, input_map, preferred_element_type=jnp.float32)
    source_pick = (deal_order[:, None] == all_stretches[None, :]).astype(jnp.float32)
    source_end = jnp.dot(source_pick, prefix, precision=lax.Precision.HIGHEST)
    source_doc = doc_index(ends, deal_order * STRETCH + STRETCH - 1)
    allowed = (deal_order[None, :] < my_stretches[:, None]) & (
        source_doc[None, :] == prev_own[:, None]
    )
    spans = jnp.exp(
        jnp.where(allowed[..., None], base_own[:, None, :] - source_end[None, :, :], -jnp.inf)
    )
    state_in = jnp.einsum(
        "ick,ckn->ikn",
        jnp.repeat(spans, HEAD_DIM, axis=2),
        lax.all_gather(states, "seq", axis=0, tiled=True),
        precision=lax.Precision.HIGHEST,
    )
    later = lane[:, None] >= lane[None, :]
    direct_gain = jnp.repeat(skip_gain, HEAD_DIM)[None, :]

    def stretch_out(inputs):
        values_c, scaled_c, keys_c, queries_c, running_c, doc_c, base_c, prev_c, state_c = inputs
        scores = jnp.dot(queries_c, keys_c.T, preferred_element_type=jnp.float32)
        same = (doc_c[:, None] == doc_c[None, :]) & later
        spans = running_c.T[:, :, None] - running_c.T[:, None, :]
        mixing = (scores[None] * jnp.exp(jnp.where(same[None], spans, -jnp.inf))).astype(
            jnp.bfloat16
        )
        within = jnp.einsum(
            "hts,shp->thp",
            mixing,
            scaled_c.reshape(STRETCH, HEADS, HEAD_DIM),
            preferred_element_type=jnp.float32,
        ).reshape(STRETCH, INNER)
        readout = jnp.dot(
            queries_c, state_c.astype(jnp.bfloat16).T, preferred_element_type=jnp.float32
        )
        carry_weight = jnp.exp(
            jnp.where((doc_c == prev_c)[:, None], running_c - base_c[None, :], -jnp.inf)
        )
        return (
            within
            + readout * jnp.repeat(carry_weight, HEAD_DIM, axis=1)
            + values_c.astype(jnp.float32) * direct_gain
        )

    outputs = lax.map(
        stretch_out,
        (values, scaled, input_map, output_map, running, own_doc, base_own, prev_own, state_in),
    )
    gated = outputs.reshape(local_rows, INNER) * jax.nn.silu(gate_input.astype(jnp.float32))
    normed = gated * lax.rsqrt(jnp.mean(gated * gated, axis=1, keepdims=True) + 1e-05) * norm_gain
    mixed_out = normed.astype(jnp.bfloat16)
    slot_numbers = jnp.arange(stretches_here, dtype=jnp.int32)

    def one_doc(document):
        last = lax.dynamic_index_in_dim(ends, document, keepdims=False) - 1
        owner = last // STRETCH
        match = my_stretches == owner
        slot = jnp.sum(jnp.where(match, slot_numbers, 0))

        def present():
            within_pos = last - owner * STRETCH
            running_c = lax.dynamic_index_in_dim(running, slot, keepdims=False)
            running_e = lax.dynamic_index_in_dim(running_c, within_pos, keepdims=False)
            doc_c = lax.dynamic_index_in_dim(own_doc, slot, keepdims=False)
            scaled_c = lax.dynamic_index_in_dim(scaled, slot, keepdims=False)
            keys_c = lax.dynamic_index_in_dim(input_map, slot, keepdims=False)
            base_c = lax.dynamic_index_in_dim(base_own, slot, keepdims=False)
            prev_c = lax.dynamic_index_in_dim(prev_own, slot, keepdims=False)
            state_c = lax.dynamic_index_in_dim(state_in, slot, keepdims=False)
            weight = jnp.exp(
                jnp.where((doc_c == document)[:, None], running_e[None, :] - running_c, -jnp.inf)
            )
            final_weighted = (
                scaled_c.astype(jnp.float32) * jnp.repeat(weight, HEAD_DIM, axis=1)
            ).astype(jnp.bfloat16)
            part = jnp.dot(final_weighted.T, keys_c, preferred_element_type=jnp.float32)
            carry_weight = jnp.exp(jnp.where(prev_c == document, running_e - base_c, -jnp.inf))
            return part + jnp.repeat(carry_weight, HEAD_DIM)[:, None] * state_c

        def absent():
            return jnp.zeros((INNER, STATE), jnp.float32)

        return lax.cond(jnp.any(match), present, absent)

    every_doc = jnp.transpose(lax.map(one_doc, jnp.arange(DOCS, dtype=jnp.int32)), (1, 0, 2))
    kept = lax.psum_scatter(
        every_doc.astype(jnp.bfloat16), "seq", scatter_dimension=0, tiled=True
    ).astype(jnp.float32)
    final_states = jnp.transpose(kept, (1, 0, 2))
    return (mixed_out, final_states)


GROUP = 4
QUARTER = INNER // GROUP
SLOT = QUARTER + STATE
PAD = 48
ROWS3 = 3 * PAD
LOG2E = 1.4426950408889634
F32 = jnp.float32
BF16 = jnp.bfloat16


def tn(a, b):
    return lax.dot_general(a, b, (((0,), (0,)), ((), ())), preferred_element_type=F32)


def nt(a, b):
    return lax.dot_general(a, b, (((1,), (1,)), ((), ())), preferred_element_type=F32)


def split3(a):
    high = a.astype(BF16)
    rest = a - high.astype(F32)
    middle = rest.astype(BF16)
    low = (rest - middle.astype(F32)).astype(BF16)
    return jnp.concatenate([high, middle, low], 0)


def head_row(shape):
    row = lax.broadcasted_iota(jnp.int32, shape, 0)
    return row - PAD * (row >= PAD).astype(jnp.int32) - PAD * (row >= 2 * PAD).astype(jnp.int32)


def silu(v):
    return v / (1.0 + jnp.exp(-v))


def softplus(v):
    u = jnp.exp(-jnp.abs(v))
    small = u * (1.0 + u * (-1.0 / 2 + u * (1.0 / 3 + u * (-1.0 / 4 + u * (1.0 / 5)))))
    return jnp.maximum(v, 0.0) + jnp.where(u < 0.03, small, jnp.log(1.0 + u))


def one_if(condition):
    return jnp.where(condition, 1.0, 0.0).astype(F32)


def kernel(
    deal,
    lengths,
    x,
    gate,
    step_raw,
    conv_weight,
    conv_bias,
    heads_in,
    norm_gain,
    out,
    finals,
    steps,
    tails,
    keys_raw,
    values_raw,
    states_in,
    staged,
    tail_f,
    lead,
    ext,
    mixed,
    masked_scores,
    y,
    slot_ext,
    slot_weighted,
    ends_state,
    trail,
    carried,
    log_run,
    step_t,
    weight_t,
    split_run,
    expand,
    keep_mask,
    send_sem,
    recv_sem,
):
    me = lax.axis_index("seq")
    partners = (3 - me, me + 1 - 2 * lax.rem(me, 2), lax.rem(me + 2, 4))
    barrier = pltpu.get_barrier_semaphore()
    for peer in partners:
        pl.semaphore_signal(
            barrier, inc=1, device_id={"seq": peer}, device_id_type=pl.DeviceIdType.MESH
        )

    eye = (
        lax.broadcasted_iota(jnp.int32, (PAD, HEADS), 0)
        == lax.broadcasted_iota(jnp.int32, (PAD, HEADS), 1)
    ).astype(BF16)
    steps[me] = nt(eye, step_raw[...]).astype(BF16)
    last = x[STRETCH - 16 :, :].astype(F32)[13:16, :]
    tail_f[0] = jnp.zeros((16, QUARTER), F32)
    for j in range(GROUP):
        tail_f[0, 3 * j : 3 * j + 3, :] = last[:, j * QUARTER : (j + 1) * QUARTER]
    tail_f[0, 12:15, 0 : 2 * STATE] = last[:, INNER:]
    tails[me] = tail_f[0].astype(BF16)
    pl.semaphore_wait(barrier, 3)

    def remote(kind, src, dst, peer, where):
        return pltpu.make_async_remote_copy(
            src_ref=src,
            dst_ref=dst,
            send_sem=send_sem.at[kind, where],
            recv_sem=recv_sem.at[kind, me],
            device_id={"seq": peer},
            device_id_type=pl.DeviceIdType.MESH,
        )

    sends = []
    for r, peer in enumerate(partners):
        sends.append(remote(0, steps.at[me], steps.at[me], peer, r))
        sends.append(remote(1, tails.at[me], tails.at[me], peer, r))
    for r, peer in enumerate(partners):
        sends.append(
            remote(2, x.at[:, pl.ds(INNER, STATE)], keys_raw.at[me], peer, r)
        )
        columns = pl.ds(pl.multiple_of(peer * QUARTER, 128), QUARTER)
        sends.append(remote(3, x.at[:, columns], values_raw.at[me], peer, r))
    for copy in sends:
        copy.start()

    def arrived(kind, buffer, slot):
        pltpu.make_async_remote_copy(
            src_ref=buffer.at[slot],
            dst_ref=buffer.at[slot],
            send_sem=send_sem.at[kind, 0],
            recv_sem=recv_sem.at[kind, slot],
            device_id={"seq": slot},
            device_id_type=pl.DeviceIdType.MESH,
        ).wait_recv()

    ends = []
    total = 0
    for d in range(DOCS):
        total = total + lengths[d]
        ends.append(total)

    def doc_of(position):
        found = 0
        for end in ends:
            found = found + (end <= position).astype(jnp.int32)
        return found

    order = [deal[i] for i in range(GROUP)]
    mine = deal[me]

    def prev_of(stretch):
        return jnp.where(stretch > 0, doc_of(stretch * STRETCH - 1), -1)

    prev_docs = [prev_of(s) for s in order]
    end_docs = [doc_of(s * STRETCH + STRETCH - 1) for s in order]

    def make_keep(stretch):
        rows = lax.broadcasted_iota(jnp.int32, (STRETCH, 128), 0) + stretch * STRETCH
        here = doc_of(rows)
        for j in range(KERNEL - 1):
            before = rows - (KERNEL - 1) + j
            keep_mask[j] = one_if((doc_of(before) == here) & (before >= 0))
        return here

    columns_head = lax.broadcasted_iota(jnp.int32, (ROWS3, INNER), 1)
    rows_head = head_row((ROWS3, INNER)) * HEAD_DIM
    expand[...] = one_if(
        (columns_head >= rows_head) & (columns_head < rows_head + HEAD_DIM)
    ).astype(BF16)

    quarter = pl.ds(pl.multiple_of(me * QUARTER, 128), QUARTER)
    keys_raw[me] = x[:, INNER : INNER + STATE]
    values_raw[me] = x[:, quarter]

    for r, peer in enumerate(partners):
        arrived(0, steps, peer)
        arrived(1, tails, peer)
    for i in range(GROUP):
        tail_f[i] = tails[i].astype(F32)
    for i in range(GROUP):
        total_tail = jnp.zeros((16, QUARTER), F32)
        for j in range(GROUP):
            if j != i:
                total_tail = total_tail + one_if(order[j] == order[i] - 1) * tail_f[j]
        lead[i] = total_tail

    step_bias = heads_in[:, 0:1]
    rate = heads_in[:, 1:2] * LOG2E
    upper = one_if(
        lax.broadcasted_iota(jnp.int32, (STRETCH, STRETCH), 0)
        <= lax.broadcasted_iota(jnp.int32, (STRETCH, STRETCH), 1)
    ).astype(BF16)
    lanes = lax.broadcasted_iota(jnp.int32, (PAD, STRETCH), 1)
    totals = []
    at_end = []
    for i in range(GROUP):
        step = softplus(steps[i].astype(F32) + step_bias)
        step_t[i] = step
        sums = jnp.dot(split3(-rate * step), upper, preferred_element_type=F32)
        run = sums[:PAD] + sums[PAD : 2 * PAD] + sums[2 * PAD :]
        log_run[i] = run
        totals.append(run[:, STRETCH - 1 : STRETCH])
        doc_lane = doc_of(lanes + order[i] * STRETCH)
        goal = jnp.zeros((PAD, STRETCH), F32)
        row_ends = []
        for d in range(DOCS):
            final = jnp.minimum(ends[d] - 1 - order[i] * STRETCH, STRETCH - 1)
            value = jnp.sum(jnp.where(lanes == final, run, 0.0), axis=1, keepdims=True)
            row_ends.append(value)
            goal = jnp.where(doc_lane == d, value, goal)
        at_end.append(row_ends)
        weight_t[i] = jnp.exp2(jnp.minimum(goal - run, 0.0))
    split_run[...] = split3(log_run[me])

    make_keep(mine)
    for j in range(GROUP):
        ext[5:8, j * QUARTER : (j + 1) * QUARTER] = lead[me, 3 * j : 3 * j + 3, :]
    ext[5:8, INNER:] = lead[me, 12:15, 0 : 2 * STATE]

    def conv(source, cols, weight_cols):
        taps = conv_weight[:, weight_cols]
        value = conv_bias[:, weight_cols] + taps[KERNEL - 1 : KERNEL] * source[8 : 8 + STRETCH, cols]
        for j in range(KERNEL - 1):
            value = value + taps[j : j + 1] * source[5 + j : 5 + j + STRETCH, cols] * keep_mask[j]
        return silu(value).astype(BF16)

    def own_chunk(c, carry):
        cols = pl.ds(pl.multiple_of(c * 128, 128), 128)
        ext[8 : 8 + STRETCH, cols] = x[:, cols].astype(F32)
        mixed[:, cols] = conv(ext, cols, cols)
        return carry

    lax.fori_loop(0, CHANNELS // 128, own_chunk, 0)

    step_rows = jnp.transpose(split3(step_t[me]).astype(F32)).astype(BF16)
    keys = mixed[:, INNER : INNER + STATE]
    queries = mixed[:, INNER + STATE :]
    t_index = lax.broadcasted_iota(jnp.int32, (STRETCH, STRETCH), 0)
    s_index = lax.broadcasted_iota(jnp.int32, (STRETCH, STRETCH), 1)
    same = (t_index >= s_index) & (
        doc_of(t_index + mine * STRETCH) == doc_of(s_index + mine * STRETCH)
    )
    scores = jnp.where(same, nt(queries, keys), 0.0)
    low_lane = lax.broadcasted_iota(jnp.int32, (STRETCH, 128), 1) < HEAD_DIM
    run_rows = jnp.transpose(split_run[...].astype(F32)).astype(BF16)
    pick_rows = head_row((ROWS3, 128))

    def pair(p, carry):
        cols = pl.ds(pl.multiple_of(p * 128, 128), 128)
        values = mixed[:, cols].astype(F32)
        spread = expand[:, cols]
        wide = (values * jnp.dot(step_rows, spread, preferred_element_type=F32)).astype(BF16)
        parts = []
        for k in range(2):
            head = 2 * p + k
            pick = one_if(pick_rows == head).astype(BF16)
            column = jnp.dot(run_rows, pick, preferred_element_type=F32)
            row = log_run[me, pl.ds(head, 1), :]
            first = masked_scores[0:128, 0:128] * jnp.exp2(
                jnp.minimum(column[0:128] - row[:, 0:128], 0.0)
            )
            top = jnp.dot(first.astype(BF16), wide[0:128], preferred_element_type=F32)
            second = jnp.concatenate(
                [
                    masked_scores[128:256, b * 128 : b * 128 + 128]
                    * jnp.exp2(
                        jnp.minimum(column[128:256] - row[:, b * 128 : b * 128 + 128], 0.0)
                    )
                    for b in range(2)
                ],
                1,
            )
            bottom = jnp.dot(second.astype(BF16), wide, preferred_element_type=F32)
            parts.append(jnp.concatenate([top, bottom], 0))
        skip = jnp.dot(skip_rows, spread, preferred_element_type=F32)[0:1]
        y[:, cols] = jnp.where(low_lane, parts[0], parts[1]) + skip * values
        return carry

    skip_split = split3(jnp.broadcast_to(heads_in[:, 2:3], (PAD, 128)))
    skip_rows = jnp.transpose(skip_split.astype(F32))[0:16].astype(BF16)
    masked_scores[...] = scores
    lax.fori_loop(0, HEADS // 2, pair, 0)

    spread_q = expand[:, quarter]
    for slot in (me,) + (partners[1], partners[2], partners[0]):
        if slot is not me:
            arrived(2, keys_raw, slot)
            arrived(3, values_raw, slot)
        stretch = deal[slot]
        here_slot = make_keep(stretch)
        for k in range(KERNEL - 1):
            slot_ext[5 + k : 6 + k, 0:QUARTER] = lead[slot, pl.ds(3 * me + k, 1), :]
        slot_ext[5:8, QUARTER:] = lead[slot, 12:15, 0:STATE]
        slot_ext[8:, QUARTER:] = keys_raw[slot].astype(F32)
        slot_keys = conv(
            slot_ext, pl.ds(QUARTER, STATE), pl.ds(INNER, STATE)
        )
        step_here = jnp.transpose(split3(step_t[slot]).astype(F32)).astype(BF16)
        weight_here = jnp.transpose(split3(weight_t[slot]).astype(F32)).astype(BF16)

        def slot_chunk(c, carry):
            cols = pl.ds(pl.multiple_of(c * 128, 128), 128)
            full = pl.ds(pl.multiple_of(me * QUARTER + c * 128, 128), 128)
            slot_ext[8:, cols] = values_raw[slot, :, cols].astype(F32)
            values = conv(slot_ext, cols, full).astype(F32)
            spread = expand[:, full]
            wide = (
                values * jnp.dot(step_here, spread, preferred_element_type=F32)
            ).astype(BF16)
            slot_weighted[:, cols] = (
                wide.astype(F32) * jnp.dot(weight_here, spread, preferred_element_type=F32)
            ).astype(BF16)
            return carry

        lax.fori_loop(0, QUARTER // 128, slot_chunk, 0)
        final_doc = doc_of(stretch * STRETCH + STRETCH - 1)
        slot_keys = slot_keys.astype(F32)
        masked = jnp.concatenate(
            [(slot_keys * one_if(here_slot == d)).astype(BF16) for d in range(DOCS)]
            + [(slot_keys * one_if(here_slot == final_doc)).astype(BF16)],
            1,
        )
        result = tn(slot_weighted[...], masked)
        for d in range(DOCS):
            ends_state[slot, d] = result[:, d * STATE : (d + 1) * STATE]
        trail[slot] = result[:, DOCS * STATE :]

    lane = lax.broadcasted_iota(jnp.int32, (PAD, 128), 1)
    weights = jnp.zeros((PAD, 128), F32)
    for c in range(GROUP):
        for e in range(GROUP):
            if e == c:
                continue
            span = jnp.zeros((PAD, 1), F32)
            for m in range(GROUP):
                if m not in (c, e):
                    span = span + one_if((order[m] > order[e]) & (order[m] < order[c])) * totals[m]
            allowed = one_if((order[e] < order[c]) & (end_docs[e] == prev_docs[c]))
            weights = jnp.where(lane == c * GROUP + e, allowed * jnp.exp2(span), weights)
    for d in range(DOCS):
        value = jnp.zeros((PAD, 1), F32)
        for c in range(GROUP):
            ends_here = (ends[d] > order[c] * STRETCH) & (ends[d] <= order[c] * STRETCH + STRETCH)
            value = value + one_if(ends_here & (prev_docs[c] == d)) * jnp.exp2(at_end[c][d])
        weights = jnp.where(lane == GROUP * GROUP + d, value, weights)
    by_row = tn(spread_q, split3(weights))
    for c in range(GROUP):
        state = jnp.zeros((QUARTER, STATE), F32)
        for e in range(GROUP):
            if e != c:
                state = state + by_row[:, c * GROUP + e : c * GROUP + e + 1] * trail[e]
        carried[c] = state
        staged[c] = state.astype(BF16)
    back = [
        remote(4, staged.at[peer], states_in.at[me], peer, r) for r, peer in enumerate(partners)
    ]
    for copy in back:
        copy.start()
    states_in[me] = staged[me]
    for d in range(DOCS):
        state = jnp.zeros((QUARTER, STATE), F32)
        inflow = jnp.zeros((QUARTER, STATE), F32)
        for c in range(GROUP):
            ends_here = one_if(
                (ends[d] > order[c] * STRETCH) & (ends[d] <= order[c] * STRETCH + STRETCH)
            )
            state = state + ends_here * ends_state[c, d]
            inflow = inflow + ends_here * carried[c]
        finals[d] = state + by_row[:, GROUP * GROUP + d : GROUP * GROUP + d + 1] * inflow

    doc_lane = doc_of(lanes + mine * STRETCH)
    carry_t = jnp.where(doc_lane == prev_of(mine), jnp.exp2(log_run[me]), 0.0)
    carry_rows = jnp.transpose(split3(carry_t).astype(F32)).astype(BF16)
    square = jnp.zeros((STRETCH, 128), F32)
    for slot in (me,) + (partners[1], partners[2], partners[0]):
        if slot is not me:
            arrived(4, states_in, slot)

        def read_chunk(c, square):
            cols = pl.ds(pl.multiple_of(slot * QUARTER + c * 128, 128), 128)
            rows = pl.ds(pl.multiple_of(c * 128, 128), 128)
            readout = nt(mixed[:, INNER + STATE :], states_in[slot, rows, :])
            carry = jnp.dot(carry_rows, expand[:, cols], preferred_element_type=F32)
            gated = (y[:, cols] + readout * carry) * silu(gate[:, cols].astype(F32))
            y[:, cols] = gated
            return square + gated * gated

        square = lax.fori_loop(0, QUARTER // 128, read_chunk, square)
    mean = jnp.sum(square, axis=1, keepdims=True) * (1.0 / INNER)
    factor = jnp.broadcast_to(lax.rsqrt(mean + 1e-05), (STRETCH, 128))

    def norm_chunk(c, carry):
        cols = pl.ds(pl.multiple_of(c * 128, 128), 128)
        out[:, cols] = (y[:, cols] * factor * norm_gain[:, cols]).astype(BF16)
        return carry

    lax.fori_loop(0, INNER // 128, norm_chunk, 0)
    for copy in sends + back:
        copy.wait_send()


def fused(
    mixer_in,
    gate_input,
    step_raw,
    lengths,
    deal_order,
    conv_weight,
    conv_bias,
    step_bias,
    decay_rate,
    skip_gain,
    norm_gain,
):
    heads_in = jnp.pad(jnp.stack([step_bias, decay_rate, skip_gain], 1), ((0, PAD - HEADS), (0, 0)))
    smem = pl.BlockSpec(memory_space=pltpu.SMEM)
    vmem = pl.BlockSpec(memory_space=pltpu.VMEM)
    return pl.pallas_call(
        kernel,
        out_shape=(
            jax.ShapeDtypeStruct((STRETCH, INNER), BF16),
            jax.ShapeDtypeStruct((DOCS, QUARTER, STATE), F32),
        ),
        in_specs=[smem, smem] + [vmem] * 7,
        out_specs=(vmem, vmem),
        scratch_shapes=[
            pltpu.VMEM((GROUP, PAD, STRETCH), BF16),
            pltpu.VMEM((GROUP, 16, QUARTER), BF16),
            pltpu.VMEM((GROUP, STRETCH, STATE), BF16),
            pltpu.VMEM((GROUP, STRETCH, QUARTER), BF16),
            pltpu.VMEM((GROUP, QUARTER, STATE), BF16),
            pltpu.VMEM((GROUP, QUARTER, STATE), BF16),
            pltpu.VMEM((GROUP, 16, QUARTER), F32),
            pltpu.VMEM((GROUP, 16, QUARTER), F32),
            pltpu.VMEM((STRETCH + 8, CHANNELS), F32),
            pltpu.VMEM((STRETCH, CHANNELS), BF16),
            pltpu.VMEM((STRETCH, STRETCH), F32),
            pltpu.VMEM((STRETCH, INNER), F32),
            pltpu.VMEM((STRETCH + 8, SLOT), F32),
            pltpu.VMEM((STRETCH, QUARTER), BF16),
            pltpu.VMEM((GROUP, DOCS, QUARTER, STATE), F32),
            pltpu.VMEM((GROUP, QUARTER, STATE), F32),
            pltpu.VMEM((GROUP, QUARTER, STATE), F32),
            pltpu.VMEM((GROUP, PAD, STRETCH), F32),
            pltpu.VMEM((GROUP, PAD, STRETCH), F32),
            pltpu.VMEM((GROUP, PAD, STRETCH), F32),
            pltpu.VMEM((ROWS3, STRETCH), BF16),
            pltpu.VMEM((ROWS3, INNER), BF16),
            pltpu.VMEM((KERNEL - 1, STRETCH, 128), F32),
            pltpu.SemaphoreType.DMA((5, GROUP)),
            pltpu.SemaphoreType.DMA((5, GROUP)),
        ],
        compiler_params=pltpu.CompilerParams(
            collective_id=0, has_side_effects=True, vmem_limit_bytes=56 * 1024 * 1024
        ),
    )(
        deal_order,
        lengths,
        mixer_in,
        gate_input,
        step_raw,
        conv_weight,
        conv_bias[None, :],
        heads_in,
        norm_gain[None, :],
    )


def solution(mesh):
    return jax.shard_map(
        fused if mesh.shape["seq"] == GROUP else body,
        mesh=mesh,
        in_specs=(
            P(("dp", "seq"), None),
            P(("dp", "seq"), None),
            P(("dp", "seq"), None),
            P("dp"),
            P("dp"),
            P(),
            P(),
            P(),
            P(),
            P(),
            P(),
        ),
        out_specs=(P(("dp", "seq"), None), P("dp", "seq", None)),
        check_vma=False,
    )
```

```python
import jax
import jax.numpy as jnp
from jax import lax
from jax.experimental import pallas as pl
from jax.experimental.pallas import tpu as pltpu
from jax.sharding import PartitionSpec as P

HEADS = 40
HEAD_DIM = 64
STATE = 128
KERNEL = 4
STRETCH = 256
DOCS = 3
INNER = 2560
CHANNELS = 2816


def doc_index(ends, positions):
    return jnp.sum((ends[None, :] <= positions[:, None]).astype(jnp.int32), axis=1)


def lower_ones(size):
    index = jnp.arange(size, dtype=jnp.int32)
    return (index[:, None] >= index[None, :]).astype(jnp.float32)


def ends_of(lengths):
    index = jnp.arange(lengths.shape[0], dtype=jnp.int32)
    return jnp.sum(jnp.where(index[:, None] >= index[None, :], lengths[None, :], 0), axis=1)


def body(
    mixer_in,
    gate_input,
    step_raw,
    lengths,
    deal_order,
    conv_weight,
    conv_bias,
    step_bias,
    decay_rate,
    skip_gain,
    norm_gain,
):
    myself = lax.axis_index("seq")
    local_rows = mixer_in.shape[0]
    stretches_here = local_rows // STRETCH
    stretch_total = deal_order.shape[0]
    ends = ends_of(lengths)
    all_stretches = jnp.arange(stretch_total, dtype=jnp.int32)
    my_stretches = lax.dynamic_slice_in_dim(deal_order, myself * stretches_here, stretches_here)
    lane = jnp.arange(STRETCH, dtype=jnp.int32)
    own_doc = doc_index(
        ends, (my_stretches[:, None] * STRETCH + lane[None, :]).reshape(-1)
    ).reshape(stretches_here, STRETCH)
    prev_own = jnp.where(my_stretches > 0, doc_index(ends, my_stretches * STRETCH - 1), -1)
    blocks_in = mixer_in.reshape(stretches_here, STRETCH, CHANNELS)
    tails = blocks_in[:, STRETCH - (KERNEL - 1) :, :]
    step_blocks = step_raw.reshape(stretches_here, STRETCH, HEADS)
    step = jax.nn.softplus(step_blocks.astype(jnp.float32) + step_bias)
    log_decay = -decay_rate * step
    all_tails, all_steps = (
        lax.all_gather(tails, "seq", axis=0, tiled=True),
        lax.all_gather(step_blocks, "seq", axis=0, tiled=True),
    )
    totals = jnp.sum(
        -decay_rate * jax.nn.softplus(all_steps.astype(jnp.float32) + step_bias), axis=1
    )
    slot_map = (deal_order[:, None] == all_stretches[None, :]).astype(jnp.float32)
    packed_totals = jnp.dot(slot_map.T, totals, precision=lax.Precision.HIGHEST)
    prefix = jnp.dot(lower_ones(stretch_total), packed_totals, precision=lax.Precision.HIGHEST)
    base = jnp.concatenate([jnp.zeros((1, HEADS), jnp.float32), prefix[:-1]], 0)
    pick_own = (my_stretches[:, None] == all_stretches[None, :]).astype(jnp.float32)
    base_own = jnp.dot(pick_own, base, precision=lax.Precision.HIGHEST)
    running = base_own[:, None, :] + jnp.einsum(
        "ts,ish->ith", lower_ones(STRETCH), log_decay, precision=lax.Precision.HIGHEST
    )
    prev_pick = (deal_order[None, :] == my_stretches[:, None] - 1).astype(jnp.bfloat16)
    prev_rows = jnp.einsum(
        "is,skc->ikc", prev_pick, all_tails, preferred_element_type=jnp.float32
    ).astype(jnp.bfloat16)
    extended = jnp.concatenate([prev_rows, blocks_in], 1)
    lead = (
        my_stretches[:, None] * STRETCH
        - (KERNEL - 1)
        + jnp.arange(KERNEL - 1, dtype=jnp.int32)[None, :]
    ).reshape(-1)
    ext_doc = jnp.concatenate(
        [doc_index(ends, lead).reshape(stretches_here, KERNEL - 1), own_doc], 1
    )
    accum = jnp.zeros((stretches_here, STRETCH, CHANNELS), jnp.float32) + conv_bias
    for offset in range(KERNEL):
        keep = (ext_doc[:, offset : offset + STRETCH] == own_doc).astype(jnp.float32)
        accum = (
            accum
            + conv_weight[offset]
            * extended[:, offset : offset + STRETCH, :].astype(jnp.float32)
            * keep[..., None]
        )
    mixed = jax.nn.silu(accum).astype(jnp.bfloat16)
    values = mixed[..., :INNER]
    input_map = mixed[..., INNER : INNER + STATE]
    output_map = mixed[..., INNER + STATE :]
    scaled = (values.astype(jnp.float32) * jnp.repeat(step, HEAD_DIM, axis=2)).astype(jnp.bfloat16)
    end_weight = jnp.exp(
        jnp.where((own_doc == own_doc[:, -1:])[..., None], running[:, -1:, :] - running, -jnp.inf)
    )
    weighted = (scaled.astype(jnp.float32) * jnp.repeat(end_weight, HEAD_DIM, axis=2)).astype(
        jnp.bfloat16
    )
    states = jnp.einsum("isk,isn->ikn", weighted, input_map, preferred_element_type=jnp.float32)
    source_pick = (deal_order[:, None] == all_stretches[None, :]).astype(jnp.float32)
    source_end = jnp.dot(source_pick, prefix, precision=lax.Precision.HIGHEST)
    source_doc = doc_index(ends, deal_order * STRETCH + STRETCH - 1)
    allowed = (deal_order[None, :] < my_stretches[:, None]) & (
        source_doc[None, :] == prev_own[:, None]
    )
    spans = jnp.exp(
        jnp.where(allowed[..., None], base_own[:, None, :] - source_end[None, :, :], -jnp.inf)
    )
    state_in = jnp.einsum(
        "ick,ckn->ikn",
        jnp.repeat(spans, HEAD_DIM, axis=2),
        lax.all_gather(states, "seq", axis=0, tiled=True),
        precision=lax.Precision.HIGHEST,
    )
    later = lane[:, None] >= lane[None, :]
    direct_gain = jnp.repeat(skip_gain, HEAD_DIM)[None, :]

    def stretch_out(inputs):
        values_c, scaled_c, keys_c, queries_c, running_c, doc_c, base_c, prev_c, state_c = inputs
        scores = jnp.dot(queries_c, keys_c.T, preferred_element_type=jnp.float32)
        same = (doc_c[:, None] == doc_c[None, :]) & later
        spans = running_c.T[:, :, None] - running_c.T[:, None, :]
        mixing = (scores[None] * jnp.exp(jnp.where(same[None], spans, -jnp.inf))).astype(
            jnp.bfloat16
        )
        within = jnp.einsum(
            "hts,shp->thp",
            mixing,
            scaled_c.reshape(STRETCH, HEADS, HEAD_DIM),
            preferred_element_type=jnp.float32,
        ).reshape(STRETCH, INNER)
        readout = jnp.dot(
            queries_c, state_c.astype(jnp.bfloat16).T, preferred_element_type=jnp.float32
        )
        carry_weight = jnp.exp(
            jnp.where((doc_c == prev_c)[:, None], running_c - base_c[None, :], -jnp.inf)
        )
        return (
            within
            + readout * jnp.repeat(carry_weight, HEAD_DIM, axis=1)
            + values_c.astype(jnp.float32) * direct_gain
        )

    outputs = lax.map(
        stretch_out,
        (values, scaled, input_map, output_map, running, own_doc, base_own, prev_own, state_in),
    )
    gated = outputs.reshape(local_rows, INNER) * jax.nn.silu(gate_input.astype(jnp.float32))
    normed = gated * lax.rsqrt(jnp.mean(gated * gated, axis=1, keepdims=True) + 1e-05) * norm_gain
    mixed_out = normed.astype(jnp.bfloat16)
    slot_numbers = jnp.arange(stretches_here, dtype=jnp.int32)

    def one_doc(document):
        last = lax.dynamic_index_in_dim(ends, document, keepdims=False) - 1
        owner = last // STRETCH
        match = my_stretches == owner
        slot = jnp.sum(jnp.where(match, slot_numbers, 0))

        def present():
            within_pos = last - owner * STRETCH
            running_c = lax.dynamic_index_in_dim(running, slot, keepdims=False)
            running_e = lax.dynamic_index_in_dim(running_c, within_pos, keepdims=False)
            doc_c = lax.dynamic_index_in_dim(own_doc, slot, keepdims=False)
            scaled_c = lax.dynamic_index_in_dim(scaled, slot, keepdims=False)
            keys_c = lax.dynamic_index_in_dim(input_map, slot, keepdims=False)
            base_c = lax.dynamic_index_in_dim(base_own, slot, keepdims=False)
            prev_c = lax.dynamic_index_in_dim(prev_own, slot, keepdims=False)
            state_c = lax.dynamic_index_in_dim(state_in, slot, keepdims=False)
            weight = jnp.exp(
                jnp.where((doc_c == document)[:, None], running_e[None, :] - running_c, -jnp.inf)
            )
            final_weighted = (
                scaled_c.astype(jnp.float32) * jnp.repeat(weight, HEAD_DIM, axis=1)
            ).astype(jnp.bfloat16)
            part = jnp.dot(final_weighted.T, keys_c, preferred_element_type=jnp.float32)
            carry_weight = jnp.exp(jnp.where(prev_c == document, running_e - base_c, -jnp.inf))
            return part + jnp.repeat(carry_weight, HEAD_DIM)[:, None] * state_c

        def absent():
            return jnp.zeros((INNER, STATE), jnp.float32)

        return lax.cond(jnp.any(match), present, absent)

    every_doc = jnp.transpose(lax.map(one_doc, jnp.arange(DOCS, dtype=jnp.int32)), (1, 0, 2))
    kept = lax.psum_scatter(
        every_doc.astype(jnp.bfloat16), "seq", scatter_dimension=0, tiled=True
    ).astype(jnp.float32)
    final_states = jnp.transpose(kept, (1, 0, 2))
    return (mixed_out, final_states)


GROUP = 4
QUARTER = INNER // GROUP
SLOT = QUARTER + STATE
PAD = 48
ROWS3 = 3 * PAD
EARLY = 10
LOG2E = 1.4426950408889634
F32 = jnp.float32
BF16 = jnp.bfloat16


def tn(a, b):
    return lax.dot_general(a, b, (((0,), (0,)), ((), ())), preferred_element_type=F32)


def nt(a, b):
    return lax.dot_general(a, b, (((1,), (1,)), ((), ())), preferred_element_type=F32)


def split3(a):
    high = a.astype(BF16)
    rest = a - high.astype(F32)
    middle = rest.astype(BF16)
    low = (rest - middle.astype(F32)).astype(BF16)
    return jnp.concatenate([high, middle, low], 0)


def head_row(shape):
    row = lax.broadcasted_iota(jnp.int32, shape, 0)
    return row - PAD * (row >= PAD).astype(jnp.int32) - PAD * (row >= 2 * PAD).astype(jnp.int32)


def silu(v):
    return v / (1.0 + jnp.exp(-v))


def softplus(v):
    u = jnp.exp(-jnp.abs(v))
    small = u * (1.0 + u * (-1.0 / 2 + u * (1.0 / 3 + u * (-1.0 / 4 + u * (1.0 / 5)))))
    return jnp.maximum(v, 0.0) + jnp.where(u < 0.03, small, jnp.log(1.0 + u))


def one_if(condition):
    return jnp.where(condition, 1.0, 0.0).astype(F32)


def kernel(
    deal,
    lengths,
    x,
    gate_hbm,
    step_raw,
    conv_weight,
    conv_bias,
    step_bias_in,
    rate_in,
    skip_in,
    norm_gain,
    out,
    finals_hbm,
    steps,
    tails,
    keys_raw,
    values_raw,
    states_in,
    staged,
    tail_f,
    lead,
    ext,
    mixed,
    masked_scores,
    y,
    slot_ext,
    slot_weighted,
    ends_state,
    trail,
    carried,
    log_run,
    step_t,
    weight_t,
    split_run,
    expand,
    keep_mask,
    params,
    per_head,
    gate,
    finals,
    local_sem,
    send_sem,
    recv_sem,
):
    me = lax.axis_index("seq")
    partners = (3 - me, me + 1 - 2 * lax.rem(me, 2), lax.rem(me + 2, 4))
    barrier = pltpu.get_barrier_semaphore()
    for peer in partners:
        pl.semaphore_signal(
            barrier, inc=1, device_id={"seq": peer}, device_id_type=pl.DeviceIdType.MESH
        )

    gate_copy = pltpu.make_async_copy(gate_hbm, gate, local_sem.at[0])
    gate_copy.start()
    finals_copy = pltpu.make_async_copy(finals, finals_hbm, local_sem.at[1])

    steps[me] = jnp.concatenate(
        [step_raw[...].astype(F32), jnp.zeros((PAD - HEADS, STRETCH), F32)], 0
    ).astype(BF16)
    last = x[STRETCH - 16 :, :].astype(F32)[13:16, :]
    tail_f[0] = jnp.zeros((16, QUARTER), F32)
    for j in range(GROUP):
        tail_f[0, 3 * j : 3 * j + 3, :] = last[:, j * QUARTER : (j + 1) * QUARTER]
    tail_f[0, 12:15, 0 : 2 * STATE] = last[:, INNER:]
    tails[me] = tail_f[0].astype(BF16)
    pl.semaphore_wait(barrier, 3)

    def remote(kind, src, dst, peer, where):
        return pltpu.make_async_remote_copy(
            src_ref=src,
            dst_ref=dst,
            send_sem=send_sem.at[kind, where],
            recv_sem=recv_sem.at[kind, me],
            device_id={"seq": peer},
            device_id_type=pl.DeviceIdType.MESH,
        )

    sends = []
    for r, peer in enumerate(partners):
        sends.append(remote(0, steps.at[me], steps.at[me], peer, r))
        sends.append(remote(1, tails.at[me], tails.at[me], peer, r))
    for r, peer in enumerate(partners):
        sends.append(
            remote(2, x.at[:, pl.ds(INNER, STATE)], keys_raw.at[me], peer, r)
        )
        columns = pl.ds(pl.multiple_of(peer * QUARTER, 128), QUARTER)
        sends.append(remote(3, x.at[:, columns], values_raw.at[me], peer, r))
    for copy in sends:
        copy.start()

    def arrived(kind, buffer, slot):
        pltpu.make_async_remote_copy(
            src_ref=buffer.at[slot],
            dst_ref=buffer.at[slot],
            send_sem=send_sem.at[kind, 0],
            recv_sem=recv_sem.at[kind, slot],
            device_id={"seq": slot},
            device_id_type=pl.DeviceIdType.MESH,
        ).wait_recv()

    ends = []
    total = 0
    for d in range(DOCS):
        total = total + lengths[d]
        ends.append(total)

    def doc_of(position):
        found = 0
        for end in ends:
            found = found + (end <= position).astype(jnp.int32)
        return found

    order = [deal[i] for i in range(GROUP)]
    mine = deal[me]

    def prev_of(stretch):
        return jnp.where(stretch > 0, doc_of(stretch * STRETCH - 1), -1)

    prev_docs = [prev_of(s) for s in order]
    end_docs = [doc_of(s * STRETCH + STRETCH - 1) for s in order]

    def make_keep(stretch):
        rows = lax.broadcasted_iota(jnp.int32, (STRETCH, 128), 0) + stretch * STRETCH
        here = doc_of(rows)
        for j in range(KERNEL - 1):
            before = rows - (KERNEL - 1) + j
            keep_mask[j] = one_if((doc_of(before) == here) & (before >= 0))
        return here

    columns_head = lax.broadcasted_iota(jnp.int32, (ROWS3, INNER), 1)
    rows_head = head_row((ROWS3, INNER)) * HEAD_DIM
    expand[...] = one_if(
        (columns_head >= rows_head) & (columns_head < rows_head + HEAD_DIM)
    ).astype(BF16)

    quarter = pl.ds(pl.multiple_of(me * QUARTER, 128), QUARTER)
    keys_raw[me] = x[:, INNER : INNER + STATE]
    values_raw[me] = x[:, quarter]

    for r, peer in enumerate(partners):
        arrived(0, steps, peer)
        arrived(1, tails, peer)
    for i in range(GROUP):
        tail_f[i] = tails[i].astype(F32)
    for i in range(GROUP):
        total_tail = jnp.zeros((16, QUARTER), F32)
        for j in range(GROUP):
            if j != i:
                total_tail = total_tail + one_if(order[j] == order[i] - 1) * tail_f[j]
        lead[i] = total_tail

    params[0:KERNEL] = conv_weight[...]
    for c in range(CHANNELS // 128):
        params[4:5, c * 128 : c * 128 + 128] = conv_bias[c * 128 : c * 128 + 128][None, :]
    for c in range(INNER // 128):
        params[5:6, c * 128 : c * 128 + 128] = norm_gain[c * 128 : c * 128 + 128][None, :]
    per_head[...] = jnp.zeros((8, 128), F32)
    for k, source in enumerate((step_bias_in, rate_in, skip_in)):
        per_head[k : k + 1, 0:HEADS] = source[...]
    heads_in = jnp.transpose(per_head[...])[0:PAD]
    step_bias = heads_in[:, 0:1]
    rate = heads_in[:, 1:2] * LOG2E
    upper = one_if(
        lax.broadcasted_iota(jnp.int32, (STRETCH, STRETCH), 0)
        <= lax.broadcasted_iota(jnp.int32, (STRETCH, STRETCH), 1)
    ).astype(BF16)
    lanes = lax.broadcasted_iota(jnp.int32, (PAD, STRETCH), 1)
    totals = []
    at_end = []
    for i in range(GROUP):
        step = softplus(steps[i].astype(F32) + step_bias)
        step_t[i] = step
        sums = jnp.dot(split3(-rate * step), upper, preferred_element_type=F32)
        run = sums[:PAD] + sums[PAD : 2 * PAD] + sums[2 * PAD :]
        log_run[i] = run
        totals.append(run[:, STRETCH - 1 : STRETCH])
        doc_lane = doc_of(lanes + order[i] * STRETCH)
        goal = jnp.zeros((PAD, STRETCH), F32)
        row_ends = []
        for d in range(DOCS):
            final = jnp.minimum(ends[d] - 1 - order[i] * STRETCH, STRETCH - 1)
            value = jnp.sum(jnp.where(lanes == final, run, 0.0), axis=1, keepdims=True)
            row_ends.append(value)
            goal = jnp.where(doc_lane == d, value, goal)
        at_end.append(row_ends)
        weight_t[i] = jnp.exp2(jnp.minimum(goal - run, 0.0))
    split_run[...] = split3(log_run[me])

    make_keep(mine)
    for j in range(GROUP):
        ext[5:8, j * QUARTER : (j + 1) * QUARTER] = lead[me, 3 * j : 3 * j + 3, :]
    ext[5:8, INNER:] = lead[me, 12:15, 0 : 2 * STATE]

    def conv(source, cols, weight_cols):
        taps = params[0:8, weight_cols]
        value = taps[4:5] + taps[KERNEL - 1 : KERNEL] * source[8 : 8 + STRETCH, cols]
        for j in range(KERNEL - 1):
            value = value + taps[j : j + 1] * source[5 + j : 5 + j + STRETCH, cols] * keep_mask[j]
        return silu(value).astype(BF16)

    def own_chunk(c, carry):
        cols = pl.ds(pl.multiple_of(c * 128, 128), 128)
        ext[8 : 8 + STRETCH, cols] = x[:, cols].astype(F32)
        mixed[:, cols] = conv(ext, cols, cols)
        return carry

    lax.fori_loop(0, CHANNELS // 128, own_chunk, 0)

    step_rows = jnp.transpose(split3(step_t[me]).astype(F32)).astype(BF16)
    keys = mixed[:, INNER : INNER + STATE]
    queries = mixed[:, INNER + STATE :]
    t_index = lax.broadcasted_iota(jnp.int32, (STRETCH, STRETCH), 0)
    s_index = lax.broadcasted_iota(jnp.int32, (STRETCH, STRETCH), 1)
    same = (t_index >= s_index) & (
        doc_of(t_index + mine * STRETCH) == doc_of(s_index + mine * STRETCH)
    )
    scores = jnp.where(same, nt(queries, keys), 0.0)
    low_lane = lax.broadcasted_iota(jnp.int32, (STRETCH, 128), 1) < HEAD_DIM
    run_rows = jnp.transpose(split_run[...].astype(F32)).astype(BF16)
    pick_rows = head_row((ROWS3, 128))

    def pair(p, carry):
        cols = pl.ds(pl.multiple_of(p * 128, 128), 128)
        values = mixed[:, cols].astype(F32)
        spread = expand[:, cols]
        wide = (values * jnp.dot(step_rows, spread, preferred_element_type=F32)).astype(BF16)
        parts = []
        for k in range(2):
            head = 2 * p + k
            pick = one_if(pick_rows == head).astype(BF16)
            column = jnp.dot(run_rows, pick, preferred_element_type=F32)
            row = log_run[me, pl.ds(head, 1), :]
            first = masked_scores[0:128, 0:128] * jnp.exp2(
                jnp.minimum(column[0:128] - row[:, 0:128], 0.0)
            )
            top = jnp.dot(first.astype(BF16), wide[0:128], preferred_element_type=F32)
            second = jnp.concatenate(
                [
                    masked_scores[128:256, b * 128 : b * 128 + 128]
                    * jnp.exp2(
                        jnp.minimum(column[128:256] - row[:, b * 128 : b * 128 + 128], 0.0)
                    )
                    for b in range(2)
                ],
                1,
            )
            bottom = jnp.dot(second.astype(BF16), wide, preferred_element_type=F32)
            parts.append(jnp.concatenate([top, bottom], 0))
        skip = jnp.dot(skip_rows, spread, preferred_element_type=F32)[0:1]
        y[:, cols] = jnp.where(low_lane, parts[0], parts[1]) + skip * values
        return carry

    skip_split = split3(jnp.broadcast_to(heads_in[:, 2:3], (PAD, 128)))
    skip_rows = jnp.transpose(skip_split.astype(F32))[0:16].astype(BF16)
    masked_scores[...] = scores
    lax.fori_loop(0, EARLY, pair, 0)

    spread_q = expand[:, quarter]
    for slot in (me,) + (partners[1], partners[2], partners[0]):
        if slot is not me:
            arrived(2, keys_raw, slot)
            arrived(3, values_raw, slot)
        stretch = deal[slot]
        here_slot = make_keep(stretch)
        for k in range(KERNEL - 1):
            slot_ext[5 + k : 6 + k, 0:QUARTER] = lead[slot, pl.ds(3 * me + k, 1), :]
        slot_ext[5:8, QUARTER:] = lead[slot, 12:15, 0:STATE]
        slot_ext[8:, QUARTER:] = keys_raw[slot].astype(F32)
        slot_keys = conv(
            slot_ext, pl.ds(QUARTER, STATE), pl.ds(INNER, STATE)
        )
        step_here = jnp.transpose(split3(step_t[slot]).astype(F32)).astype(BF16)
        weight_here = jnp.transpose(split3(weight_t[slot]).astype(F32)).astype(BF16)

        def slot_chunk(c, carry):
            cols = pl.ds(pl.multiple_of(c * 128, 128), 128)
            full = pl.ds(pl.multiple_of(me * QUARTER + c * 128, 128), 128)
            slot_ext[8:, cols] = values_raw[slot, :, cols].astype(F32)
            values = conv(slot_ext, cols, full).astype(F32)
            spread = expand[:, full]
            wide = (
                values * jnp.dot(step_here, spread, preferred_element_type=F32)
            ).astype(BF16)
            slot_weighted[:, cols] = (
                wide.astype(F32) * jnp.dot(weight_here, spread, preferred_element_type=F32)
            ).astype(BF16)
            return carry

        lax.fori_loop(0, QUARTER // 128, slot_chunk, 0)
        final_doc = doc_of(stretch * STRETCH + STRETCH - 1)
        slot_keys = slot_keys.astype(F32)
        masked = jnp.concatenate(
            [(slot_keys * one_if(here_slot == d)).astype(BF16) for d in range(DOCS)]
            + [(slot_keys * one_if(here_slot == final_doc)).astype(BF16)],
            1,
        )
        result = tn(slot_weighted[...], masked)
        for d in range(DOCS):
            ends_state[slot, d] = result[:, d * STATE : (d + 1) * STATE]
        trail[slot] = result[:, DOCS * STATE :]

    lane = lax.broadcasted_iota(jnp.int32, (PAD, 128), 1)
    weights = jnp.zeros((PAD, 128), F32)
    for c in range(GROUP):
        for e in range(GROUP):
            if e == c:
                continue
            span = jnp.zeros((PAD, 1), F32)
            for m in range(GROUP):
                if m not in (c, e):
                    span = span + one_if((order[m] > order[e]) & (order[m] < order[c])) * totals[m]
            allowed = one_if((order[e] < order[c]) & (end_docs[e] == prev_docs[c]))
            weights = jnp.where(lane == c * GROUP + e, allowed * jnp.exp2(span), weights)
    for d in range(DOCS):
        value = jnp.zeros((PAD, 1), F32)
        for c in range(GROUP):
            ends_here = (ends[d] > order[c] * STRETCH) & (ends[d] <= order[c] * STRETCH + STRETCH)
            value = value + one_if(ends_here & (prev_docs[c] == d)) * jnp.exp2(at_end[c][d])
        weights = jnp.where(lane == GROUP * GROUP + d, value, weights)
    by_row = tn(spread_q, split3(weights))
    for c in range(GROUP):
        state = jnp.zeros((QUARTER, STATE), F32)
        for e in range(GROUP):
            if e != c:
                state = state + by_row[:, c * GROUP + e : c * GROUP + e + 1] * trail[e]
        carried[c] = state
        staged[c] = state.astype(BF16)
    back = [
        remote(4, staged.at[peer], states_in.at[me], peer, r) for r, peer in enumerate(partners)
    ]
    for copy in back:
        copy.start()
    states_in[me] = staged[me]
    for d in range(DOCS):
        state = jnp.zeros((QUARTER, STATE), F32)
        inflow = jnp.zeros((QUARTER, STATE), F32)
        for c in range(GROUP):
            ends_here = one_if(
                (ends[d] > order[c] * STRETCH) & (ends[d] <= order[c] * STRETCH + STRETCH)
            )
            state = state + ends_here * ends_state[c, d]
            inflow = inflow + ends_here * carried[c]
        finals[d] = state + by_row[:, GROUP * GROUP + d : GROUP * GROUP + d + 1] * inflow

    finals_copy.start()
    lax.fori_loop(EARLY, HEADS // 2, pair, 0)

    gate_copy.wait()
    doc_lane = doc_of(lanes + mine * STRETCH)
    carry_t = jnp.where(doc_lane == prev_of(mine), jnp.exp2(log_run[me]), 0.0)
    carry_rows = jnp.transpose(split3(carry_t).astype(F32)).astype(BF16)
    square = jnp.zeros((STRETCH, 128), F32)
    for slot in (me,) + (partners[1], partners[2], partners[0]):
        if slot is not me:
            arrived(4, states_in, slot)

        def read_chunk(c, square):
            cols = pl.ds(pl.multiple_of(slot * QUARTER + c * 128, 128), 128)
            rows = pl.ds(pl.multiple_of(c * 128, 128), 128)
            readout = nt(mixed[:, INNER + STATE :], states_in[slot, rows, :])
            carry = jnp.dot(carry_rows, expand[:, cols], preferred_element_type=F32)
            gated = (y[:, cols] + readout * carry) * silu(gate[:, cols].astype(F32))
            y[:, cols] = gated
            return square + gated * gated

        square = lax.fori_loop(0, QUARTER // 128, read_chunk, square)
    mean = jnp.sum(square, axis=1, keepdims=True) * (1.0 / INNER)
    factor = jnp.broadcast_to(lax.rsqrt(mean + 1e-05), (STRETCH, 128))

    def norm_chunk(c, carry):
        cols = pl.ds(pl.multiple_of(c * 128, 128), 128)
        out[:, cols] = (y[:, cols] * factor * params[5:6, cols]).astype(BF16)
        return carry

    lax.fori_loop(0, INNER // 128, norm_chunk, 0)
    finals_copy.wait()
    for copy in sends + back:
        copy.wait_send()


def fused(
    mixer_in,
    gate_input,
    step_raw,
    lengths,
    deal_order,
    conv_weight,
    conv_bias,
    step_bias,
    decay_rate,
    skip_gain,
    norm_gain,
):
    smem = pl.BlockSpec(memory_space=pltpu.SMEM)
    vmem = pl.BlockSpec(memory_space=pltpu.VMEM)
    anywhere = pl.BlockSpec(memory_space=pl.ANY)
    return pl.pallas_call(
        kernel,
        out_shape=(
            jax.ShapeDtypeStruct((STRETCH, INNER), BF16),
            jax.ShapeDtypeStruct((DOCS, QUARTER, STATE), F32),
        ),
        in_specs=[smem, smem, vmem, anywhere] + [vmem] * 7,
        out_specs=(vmem, anywhere),
        scratch_shapes=[
            pltpu.VMEM((GROUP, PAD, STRETCH), BF16),
            pltpu.VMEM((GROUP, 16, QUARTER), BF16),
            pltpu.VMEM((GROUP, STRETCH, STATE), BF16),
            pltpu.VMEM((GROUP, STRETCH, QUARTER), BF16),
            pltpu.VMEM((GROUP, QUARTER, STATE), BF16),
            pltpu.VMEM((GROUP, QUARTER, STATE), BF16),
            pltpu.VMEM((GROUP, 16, QUARTER), F32),
            pltpu.VMEM((GROUP, 16, QUARTER), F32),
            pltpu.VMEM((STRETCH + 8, CHANNELS), F32),
            pltpu.VMEM((STRETCH, CHANNELS), BF16),
            pltpu.VMEM((STRETCH, STRETCH), F32),
            pltpu.VMEM((STRETCH, INNER), F32),
            pltpu.VMEM((STRETCH + 8, SLOT), F32),
            pltpu.VMEM((STRETCH, QUARTER), BF16),
            pltpu.VMEM((GROUP, DOCS, QUARTER, STATE), F32),
            pltpu.VMEM((GROUP, QUARTER, STATE), F32),
            pltpu.VMEM((GROUP, QUARTER, STATE), F32),
            pltpu.VMEM((GROUP, PAD, STRETCH), F32),
            pltpu.VMEM((GROUP, PAD, STRETCH), F32),
            pltpu.VMEM((GROUP, PAD, STRETCH), F32),
            pltpu.VMEM((ROWS3, STRETCH), BF16),
            pltpu.VMEM((ROWS3, INNER), BF16),
            pltpu.VMEM((KERNEL - 1, STRETCH, 128), F32),
            pltpu.VMEM((8, CHANNELS), F32),
            pltpu.VMEM((8, 128), F32),
            pltpu.VMEM((STRETCH, INNER), BF16),
            pltpu.VMEM((DOCS, QUARTER, STATE), F32),
            pltpu.SemaphoreType.DMA((2,)),
            pltpu.SemaphoreType.DMA((5, GROUP)),
            pltpu.SemaphoreType.DMA((5, GROUP)),
        ],
        compiler_params=pltpu.CompilerParams(
            collective_id=0, has_side_effects=True, vmem_limit_bytes=56 * 1024 * 1024
        ),
    )(
        deal_order,
        lengths,
        mixer_in,
        gate_input,
        step_raw.T,
        conv_weight,
        conv_bias,
        step_bias[None, :],
        decay_rate[None, :],
        skip_gain[None, :],
        norm_gain,
    )


def solution(mesh):
    return jax.shard_map(
        fused if mesh.shape["seq"] == GROUP else body,
        mesh=mesh,
        in_specs=(
            P(("dp", "seq"), None),
            P(("dp", "seq"), None),
            P(("dp", "seq"), None),
            P("dp"),
            P("dp"),
            P(),
            P(),
            P(),
            P(),
            P(),
            P(),
        ),
        out_specs=(P(("dp", "seq"), None), P("dp", "seq", None)),
        check_vma=False,
    )
```

```python
import jax
import jax.numpy as jnp
from jax import lax
from jax.experimental import pallas as pl
from jax.experimental.pallas import tpu as pltpu
from jax.sharding import PartitionSpec as P

HEADS = 40
HEAD_DIM = 64
STATE = 128
KERNEL = 4
STRETCH = 256
DOCS = 3
INNER = 2560
CHANNELS = 2816


def doc_index(ends, positions):
    return jnp.sum((ends[None, :] <= positions[:, None]).astype(jnp.int32), axis=1)


def lower_ones(size):
    index = jnp.arange(size, dtype=jnp.int32)
    return (index[:, None] >= index[None, :]).astype(jnp.float32)


def ends_of(lengths):
    index = jnp.arange(lengths.shape[0], dtype=jnp.int32)
    return jnp.sum(jnp.where(index[:, None] >= index[None, :], lengths[None, :], 0), axis=1)


def body(
    mixer_in,
    gate_input,
    step_raw,
    lengths,
    deal_order,
    conv_weight,
    conv_bias,
    step_bias,
    decay_rate,
    skip_gain,
    norm_gain,
):
    myself = lax.axis_index("seq")
    local_rows = mixer_in.shape[0]
    stretches_here = local_rows // STRETCH
    stretch_total = deal_order.shape[0]
    ends = ends_of(lengths)
    all_stretches = jnp.arange(stretch_total, dtype=jnp.int32)
    my_stretches = lax.dynamic_slice_in_dim(deal_order, myself * stretches_here, stretches_here)
    lane = jnp.arange(STRETCH, dtype=jnp.int32)
    own_doc = doc_index(
        ends, (my_stretches[:, None] * STRETCH + lane[None, :]).reshape(-1)
    ).reshape(stretches_here, STRETCH)
    prev_own = jnp.where(my_stretches > 0, doc_index(ends, my_stretches * STRETCH - 1), -1)
    blocks_in = mixer_in.reshape(stretches_here, STRETCH, CHANNELS)
    tails = blocks_in[:, STRETCH - (KERNEL - 1) :, :]
    step_blocks = step_raw.reshape(stretches_here, STRETCH, HEADS)
    step = jax.nn.softplus(step_blocks.astype(jnp.float32) + step_bias)
    log_decay = -decay_rate * step
    all_tails, all_steps = (
        lax.all_gather(tails, "seq", axis=0, tiled=True),
        lax.all_gather(step_blocks, "seq", axis=0, tiled=True),
    )
    totals = jnp.sum(
        -decay_rate * jax.nn.softplus(all_steps.astype(jnp.float32) + step_bias), axis=1
    )
    slot_map = (deal_order[:, None] == all_stretches[None, :]).astype(jnp.float32)
    packed_totals = jnp.dot(slot_map.T, totals, precision=lax.Precision.HIGHEST)
    prefix = jnp.dot(lower_ones(stretch_total), packed_totals, precision=lax.Precision.HIGHEST)
    base = jnp.concatenate([jnp.zeros((1, HEADS), jnp.float32), prefix[:-1]], 0)
    pick_own = (my_stretches[:, None] == all_stretches[None, :]).astype(jnp.float32)
    base_own = jnp.dot(pick_own, base, precision=lax.Precision.HIGHEST)
    running = base_own[:, None, :] + jnp.einsum(
        "ts,ish->ith", lower_ones(STRETCH), log_decay, precision=lax.Precision.HIGHEST
    )
    prev_pick = (deal_order[None, :] == my_stretches[:, None] - 1).astype(jnp.bfloat16)
    prev_rows = jnp.einsum(
        "is,skc->ikc", prev_pick, all_tails, preferred_element_type=jnp.float32
    ).astype(jnp.bfloat16)
    extended = jnp.concatenate([prev_rows, blocks_in], 1)
    lead = (
        my_stretches[:, None] * STRETCH
        - (KERNEL - 1)
        + jnp.arange(KERNEL - 1, dtype=jnp.int32)[None, :]
    ).reshape(-1)
    ext_doc = jnp.concatenate(
        [doc_index(ends, lead).reshape(stretches_here, KERNEL - 1), own_doc], 1
    )
    accum = jnp.zeros((stretches_here, STRETCH, CHANNELS), jnp.float32) + conv_bias
    for offset in range(KERNEL):
        keep = (ext_doc[:, offset : offset + STRETCH] == own_doc).astype(jnp.float32)
        accum = (
            accum
            + conv_weight[offset]
            * extended[:, offset : offset + STRETCH, :].astype(jnp.float32)
            * keep[..., None]
        )
    mixed = jax.nn.silu(accum).astype(jnp.bfloat16)
    values = mixed[..., :INNER]
    input_map = mixed[..., INNER : INNER + STATE]
    output_map = mixed[..., INNER + STATE :]
    scaled = (values.astype(jnp.float32) * jnp.repeat(step, HEAD_DIM, axis=2)).astype(jnp.bfloat16)
    end_weight = jnp.exp(
        jnp.where((own_doc == own_doc[:, -1:])[..., None], running[:, -1:, :] - running, -jnp.inf)
    )
    weighted = (scaled.astype(jnp.float32) * jnp.repeat(end_weight, HEAD_DIM, axis=2)).astype(
        jnp.bfloat16
    )
    states = jnp.einsum("isk,isn->ikn", weighted, input_map, preferred_element_type=jnp.float32)
    source_pick = (deal_order[:, None] == all_stretches[None, :]).astype(jnp.float32)
    source_end = jnp.dot(source_pick, prefix, precision=lax.Precision.HIGHEST)
    source_doc = doc_index(ends, deal_order * STRETCH + STRETCH - 1)
    allowed = (deal_order[None, :] < my_stretches[:, None]) & (
        source_doc[None, :] == prev_own[:, None]
    )
    spans = jnp.exp(
        jnp.where(allowed[..., None], base_own[:, None, :] - source_end[None, :, :], -jnp.inf)
    )
    state_in = jnp.einsum(
        "ick,ckn->ikn",
        jnp.repeat(spans, HEAD_DIM, axis=2),
        lax.all_gather(states, "seq", axis=0, tiled=True),
        precision=lax.Precision.HIGHEST,
    )
    later = lane[:, None] >= lane[None, :]
    direct_gain = jnp.repeat(skip_gain, HEAD_DIM)[None, :]

    def stretch_out(inputs):
        values_c, scaled_c, keys_c, queries_c, running_c, doc_c, base_c, prev_c, state_c = inputs
        scores = jnp.dot(queries_c, keys_c.T, preferred_element_type=jnp.float32)
        same = (doc_c[:, None] == doc_c[None, :]) & later
        spans = running_c.T[:, :, None] - running_c.T[:, None, :]
        mixing = (scores[None] * jnp.exp(jnp.where(same[None], spans, -jnp.inf))).astype(
            jnp.bfloat16
        )
        within = jnp.einsum(
            "hts,shp->thp",
            mixing,
            scaled_c.reshape(STRETCH, HEADS, HEAD_DIM),
            preferred_element_type=jnp.float32,
        ).reshape(STRETCH, INNER)
        readout = jnp.dot(
            queries_c, state_c.astype(jnp.bfloat16).T, preferred_element_type=jnp.float32
        )
        carry_weight = jnp.exp(
            jnp.where((doc_c == prev_c)[:, None], running_c - base_c[None, :], -jnp.inf)
        )
        return (
            within
            + readout * jnp.repeat(carry_weight, HEAD_DIM, axis=1)
            + values_c.astype(jnp.float32) * direct_gain
        )

    outputs = lax.map(
        stretch_out,
        (values, scaled, input_map, output_map, running, own_doc, base_own, prev_own, state_in),
    )
    gated = outputs.reshape(local_rows, INNER) * jax.nn.silu(gate_input.astype(jnp.float32))
    normed = gated * lax.rsqrt(jnp.mean(gated * gated, axis=1, keepdims=True) + 1e-05) * norm_gain
    mixed_out = normed.astype(jnp.bfloat16)
    slot_numbers = jnp.arange(stretches_here, dtype=jnp.int32)

    def one_doc(document):
        last = lax.dynamic_index_in_dim(ends, document, keepdims=False) - 1
        owner = last // STRETCH
        match = my_stretches == owner
        slot = jnp.sum(jnp.where(match, slot_numbers, 0))

        def present():
            within_pos = last - owner * STRETCH
            running_c = lax.dynamic_index_in_dim(running, slot, keepdims=False)
            running_e = lax.dynamic_index_in_dim(running_c, within_pos, keepdims=False)
            doc_c = lax.dynamic_index_in_dim(own_doc, slot, keepdims=False)
            scaled_c = lax.dynamic_index_in_dim(scaled, slot, keepdims=False)
            keys_c = lax.dynamic_index_in_dim(input_map, slot, keepdims=False)
            base_c = lax.dynamic_index_in_dim(base_own, slot, keepdims=False)
            prev_c = lax.dynamic_index_in_dim(prev_own, slot, keepdims=False)
            state_c = lax.dynamic_index_in_dim(state_in, slot, keepdims=False)
            weight = jnp.exp(
                jnp.where((doc_c == document)[:, None], running_e[None, :] - running_c, -jnp.inf)
            )
            final_weighted = (
                scaled_c.astype(jnp.float32) * jnp.repeat(weight, HEAD_DIM, axis=1)
            ).astype(jnp.bfloat16)
            part = jnp.dot(final_weighted.T, keys_c, preferred_element_type=jnp.float32)
            carry_weight = jnp.exp(jnp.where(prev_c == document, running_e - base_c, -jnp.inf))
            return part + jnp.repeat(carry_weight, HEAD_DIM)[:, None] * state_c

        def absent():
            return jnp.zeros((INNER, STATE), jnp.float32)

        return lax.cond(jnp.any(match), present, absent)

    every_doc = jnp.transpose(lax.map(one_doc, jnp.arange(DOCS, dtype=jnp.int32)), (1, 0, 2))
    kept = lax.psum_scatter(
        every_doc.astype(jnp.bfloat16), "seq", scatter_dimension=0, tiled=True
    ).astype(jnp.float32)
    final_states = jnp.transpose(kept, (1, 0, 2))
    return (mixed_out, final_states)


GROUP = 4
QUARTER = INNER // GROUP
SLOT = QUARTER + STATE
PAD = 48
ROWS3 = 3 * PAD
EARLY = 10
LOG2E = 1.4426950408889634
F32 = jnp.float32
BF16 = jnp.bfloat16


def tn(a, b):
    return lax.dot_general(a, b, (((0,), (0,)), ((), ())), preferred_element_type=F32)


def nt(a, b):
    return lax.dot_general(a, b, (((1,), (1,)), ((), ())), preferred_element_type=F32)


def split3(a):
    high = a.astype(BF16)
    rest = a - high.astype(F32)
    middle = rest.astype(BF16)
    low = (rest - middle.astype(F32)).astype(BF16)
    return jnp.concatenate([high, middle, low], 0)


def head_row(shape):
    row = lax.broadcasted_iota(jnp.int32, shape, 0)
    return row - PAD * (row >= PAD).astype(jnp.int32) - PAD * (row >= 2 * PAD).astype(jnp.int32)


def silu(v):
    return v / (1.0 + jnp.exp(-v))


def softplus(v):
    u = jnp.exp(-jnp.abs(v))
    small = u * (1.0 + u * (-1.0 / 2 + u * (1.0 / 3 + u * (-1.0 / 4 + u * (1.0 / 5)))))
    return jnp.maximum(v, 0.0) + jnp.where(u < 0.03, small, jnp.log(1.0 + u))


def one_if(condition):
    return jnp.where(condition, 1.0, 0.0).astype(F32)


def kernel(
    deal,
    lengths,
    x,
    gate_hbm,
    step_raw,
    conv_weight,
    conv_bias,
    step_bias_in,
    rate_in,
    skip_in,
    norm_gain,
    out,
    finals_hbm,
    steps,
    tails,
    keys_raw,
    values_raw,
    states_in,
    staged,
    tail_f,
    lead,
    ext,
    mixed,
    masked_scores,
    y,
    slot_ext,
    slot_weighted,
    ends_state,
    trail,
    carried,
    log_run,
    step_t,
    weight_t,
    split_run,
    expand,
    keep_mask,
    params,
    per_head,
    gate,
    finals,
    local_sem,
    send_sem,
    recv_sem,
):
    me = lax.axis_index("seq")
    partners = (3 - me, me + 1 - 2 * lax.rem(me, 2), lax.rem(me + 2, 4))
    barrier = pltpu.get_barrier_semaphore()
    for peer in partners:
        pl.semaphore_signal(
            barrier, inc=1, device_id={"seq": peer}, device_id_type=pl.DeviceIdType.MESH
        )

    gate_copy = pltpu.make_async_copy(gate_hbm, gate, local_sem.at[0])
    gate_copy.start()
    finals_copy = pltpu.make_async_copy(finals, finals_hbm, local_sem.at[1])

    steps[me] = jnp.concatenate(
        [step_raw[...].astype(F32), jnp.zeros((PAD - HEADS, STRETCH), F32)], 0
    ).astype(BF16)
    last = x[STRETCH - 16 :, :].astype(F32)[13:16, :]
    tail_f[0] = jnp.zeros((16, QUARTER), F32)
    for j in range(GROUP):
        tail_f[0, 3 * j : 3 * j + 3, :] = last[:, j * QUARTER : (j + 1) * QUARTER]
    tail_f[0, 12:15, 0 : 2 * STATE] = last[:, INNER:]
    tails[me] = tail_f[0].astype(BF16)
    pl.semaphore_wait(barrier, 3)

    def remote(kind, src, dst, peer, where):
        return pltpu.make_async_remote_copy(
            src_ref=src,
            dst_ref=dst,
            send_sem=send_sem.at[kind, where],
            recv_sem=recv_sem.at[kind, me],
            device_id={"seq": peer},
            device_id_type=pl.DeviceIdType.MESH,
        )

    sends = []
    for r, peer in enumerate(partners):
        sends.append(remote(0, steps.at[me], steps.at[me], peer, r))
        sends.append(remote(1, tails.at[me], tails.at[me], peer, r))
    for r, peer in enumerate(partners):
        sends.append(
            remote(2, x.at[:, pl.ds(INNER, STATE)], keys_raw.at[me], peer, r)
        )
        columns = pl.ds(pl.multiple_of(peer * QUARTER, 128), QUARTER)
        sends.append(remote(3, x.at[:, columns], values_raw.at[me], peer, r))
    for copy in sends:
        copy.start()

    def arrived(kind, buffer, slot):
        pltpu.make_async_remote_copy(
            src_ref=buffer.at[slot],
            dst_ref=buffer.at[slot],
            send_sem=send_sem.at[kind, 0],
            recv_sem=recv_sem.at[kind, slot],
            device_id={"seq": slot},
            device_id_type=pl.DeviceIdType.MESH,
        ).wait_recv()

    ends = []
    total = 0
    for d in range(DOCS):
        total = total + lengths[d]
        ends.append(total)

    def doc_of(position):
        found = 0
        for end in ends:
            found = found + (end <= position).astype(jnp.int32)
        return found

    order = [deal[i] for i in range(GROUP)]
    mine = deal[me]

    def prev_of(stretch):
        return jnp.where(stretch > 0, doc_of(stretch * STRETCH - 1), -1)

    prev_docs = [prev_of(s) for s in order]
    end_docs = [doc_of(s * STRETCH + STRETCH - 1) for s in order]

    def make_keep(stretch):
        rows = lax.broadcasted_iota(jnp.int32, (STRETCH, 128), 0) + stretch * STRETCH
        here = doc_of(rows)
        for j in range(KERNEL - 1):
            before = rows - (KERNEL - 1) + j
            keep_mask[j] = one_if((doc_of(before) == here) & (before >= 0))
        return here

    columns_head = lax.broadcasted_iota(jnp.int32, (ROWS3, INNER), 1)
    rows_head = head_row((ROWS3, INNER)) * HEAD_DIM
    expand[...] = one_if(
        (columns_head >= rows_head) & (columns_head < rows_head + HEAD_DIM)
    ).astype(BF16)

    quarter = pl.ds(pl.multiple_of(me * QUARTER, 128), QUARTER)
    keys_raw[me] = x[:, INNER : INNER + STATE]
    values_raw[me] = x[:, quarter]

    for r, peer in enumerate(partners):
        arrived(0, steps, peer)
        arrived(1, tails, peer)
    for i in range(GROUP):
        tail_f[i] = tails[i].astype(F32)
    for i in range(GROUP):
        total_tail = jnp.zeros((16, QUARTER), F32)
        for j in range(GROUP):
            if j != i:
                total_tail = total_tail + one_if(order[j] == order[i] - 1) * tail_f[j]
        lead[i] = total_tail

    params[0:KERNEL] = conv_weight[...]
    for c in range(CHANNELS // 128):
        params[4:5, c * 128 : c * 128 + 128] = conv_bias[c * 128 : c * 128 + 128][None, :]
    for c in range(INNER // 128):
        params[5:6, c * 128 : c * 128 + 128] = norm_gain[c * 128 : c * 128 + 128][None, :]
    per_head[...] = jnp.zeros((8, 128), F32)
    for k, source in enumerate((step_bias_in, rate_in, skip_in)):
        per_head[k : k + 1, 0:HEADS] = source[...]
    heads_in = jnp.transpose(per_head[...])[0:PAD]
    step_bias = heads_in[:, 0:1]
    rate = heads_in[:, 1:2] * LOG2E
    upper = one_if(
        lax.broadcasted_iota(jnp.int32, (STRETCH, STRETCH), 0)
        <= lax.broadcasted_iota(jnp.int32, (STRETCH, STRETCH), 1)
    ).astype(BF16)
    lanes = lax.broadcasted_iota(jnp.int32, (PAD, STRETCH), 1)
    totals = []
    at_end = []
    for i in range(GROUP):
        step = softplus(steps[i].astype(F32) + step_bias)
        step_t[i] = step
        sums = jnp.dot(split3(-rate * step), upper, preferred_element_type=F32)
        run = sums[:PAD] + sums[PAD : 2 * PAD] + sums[2 * PAD :]
        log_run[i] = run
        totals.append(run[:, STRETCH - 1 : STRETCH])
        doc_lane = doc_of(lanes + order[i] * STRETCH)
        goal = jnp.zeros((PAD, STRETCH), F32)
        row_ends = []
        for d in range(DOCS):
            final = jnp.minimum(ends[d] - 1 - order[i] * STRETCH, STRETCH - 1)
            value = jnp.sum(jnp.where(lanes == final, run, 0.0), axis=1, keepdims=True)
            row_ends.append(value)
            goal = jnp.where(doc_lane == d, value, goal)
        at_end.append(row_ends)
        weight_t[i] = jnp.exp2(jnp.minimum(goal - run, 0.0))
    split_run[...] = split3(log_run[me])

    make_keep(mine)
    for j in range(GROUP):
        ext[5:8, j * QUARTER : (j + 1) * QUARTER] = lead[me, 3 * j : 3 * j + 3, :]
    ext[5:8, INNER:] = lead[me, 12:15, 0 : 2 * STATE]

    def conv(source, cols, weight_cols):
        taps = params[0:8, weight_cols]
        value = taps[4:5] + taps[KERNEL - 1 : KERNEL] * source[8 : 8 + STRETCH, cols]
        for j in range(KERNEL - 1):
            value = value + taps[j : j + 1] * source[5 + j : 5 + j + STRETCH, cols] * keep_mask[j]
        return silu(value).astype(BF16)

    def own_chunk(c, carry):
        cols = pl.ds(pl.multiple_of(c * 128, 128), 128)
        ext[8 : 8 + STRETCH, cols] = x[:, cols].astype(F32)
        mixed[:, cols] = conv(ext, cols, cols)
        return carry

    lax.fori_loop(0, CHANNELS // 128, own_chunk, 0, unroll=2)

    step_rows = jnp.transpose(split3(step_t[me]).astype(F32)).astype(BF16)
    keys = mixed[:, INNER : INNER + STATE]
    queries = mixed[:, INNER + STATE :]
    t_index = lax.broadcasted_iota(jnp.int32, (STRETCH, STRETCH), 0)
    s_index = lax.broadcasted_iota(jnp.int32, (STRETCH, STRETCH), 1)
    same = (t_index >= s_index) & (
        doc_of(t_index + mine * STRETCH) == doc_of(s_index + mine * STRETCH)
    )
    scores = jnp.where(same, nt(queries, keys), 0.0)
    low_lane = lax.broadcasted_iota(jnp.int32, (STRETCH, 128), 1) < HEAD_DIM
    run_rows = jnp.transpose(split_run[...].astype(F32)).astype(BF16)
    pick_rows = head_row((ROWS3, 128))

    def pair(p, carry):
        cols = pl.ds(pl.multiple_of(p * 128, 128), 128)
        values = mixed[:, cols].astype(F32)
        spread = expand[:, cols]
        wide = (values * jnp.dot(step_rows, spread, preferred_element_type=F32)).astype(BF16)
        parts = []
        for k in range(2):
            head = 2 * p + k
            pick = one_if(pick_rows == head).astype(BF16)
            column = jnp.dot(run_rows, pick, preferred_element_type=F32)
            row = log_run[me, pl.ds(head, 1), :]
            first = masked_scores[0:128, 0:128] * jnp.exp2(
                jnp.minimum(column[0:128] - row[:, 0:128], 0.0)
            )
            top = jnp.dot(first.astype(BF16), wide[0:128], preferred_element_type=F32)
            second = jnp.concatenate(
                [
                    masked_scores[128:256, b * 128 : b * 128 + 128]
                    * jnp.exp2(
                        jnp.minimum(column[128:256] - row[:, b * 128 : b * 128 + 128], 0.0)
                    )
                    for b in range(2)
                ],
                1,
            )
            bottom = jnp.dot(second.astype(BF16), wide, preferred_element_type=F32)
            parts.append(jnp.concatenate([top, bottom], 0))
        skip = jnp.dot(skip_rows, spread, preferred_element_type=F32)[0:1]
        y[:, cols] = jnp.where(low_lane, parts[0], parts[1]) + skip * values
        return carry

    skip_split = split3(jnp.broadcast_to(heads_in[:, 2:3], (PAD, 128)))
    skip_rows = jnp.transpose(skip_split.astype(F32))[0:16].astype(BF16)
    masked_scores[...] = scores
    lax.fori_loop(0, EARLY, pair, 0, unroll=2)

    spread_q = expand[:, quarter]
    for slot in (me,) + (partners[1], partners[2], partners[0]):
        if slot is not me:
            arrived(2, keys_raw, slot)
            arrived(3, values_raw, slot)
        stretch = deal[slot]
        here_slot = make_keep(stretch)
        for k in range(KERNEL - 1):
            slot_ext[5 + k : 6 + k, 0:QUARTER] = lead[slot, pl.ds(3 * me + k, 1), :]
        slot_ext[5:8, QUARTER:] = lead[slot, 12:15, 0:STATE]
        slot_ext[8:, QUARTER:] = keys_raw[slot].astype(F32)
        slot_keys = conv(
            slot_ext, pl.ds(QUARTER, STATE), pl.ds(INNER, STATE)
        )
        step_here = jnp.transpose(split3(step_t[slot]).astype(F32)).astype(BF16)
        weight_here = jnp.transpose(split3(weight_t[slot]).astype(F32)).astype(BF16)

        def slot_chunk(c, carry):
            cols = pl.ds(pl.multiple_of(c * 128, 128), 128)
            full = pl.ds(pl.multiple_of(me * QUARTER + c * 128, 128), 128)
            slot_ext[8:, cols] = values_raw[slot, :, cols].astype(F32)
            values = conv(slot_ext, cols, full).astype(F32)
            spread = expand[:, full]
            wide = (
                values * jnp.dot(step_here, spread, preferred_element_type=F32)
            ).astype(BF16)
            slot_weighted[:, cols] = (
                wide.astype(F32) * jnp.dot(weight_here, spread, preferred_element_type=F32)
            ).astype(BF16)
            return carry

        lax.fori_loop(0, QUARTER // 128, slot_chunk, 0)
        final_doc = doc_of(stretch * STRETCH + STRETCH - 1)
        slot_keys = slot_keys.astype(F32)
        masked = jnp.concatenate(
            [(slot_keys * one_if(here_slot == d)).astype(BF16) for d in range(DOCS)]
            + [(slot_keys * one_if(here_slot == final_doc)).astype(BF16)],
            1,
        )
        result = tn(slot_weighted[...], masked)
        for d in range(DOCS):
            ends_state[slot, d] = result[:, d * STATE : (d + 1) * STATE]
        trail[slot] = result[:, DOCS * STATE :]

    lane = lax.broadcasted_iota(jnp.int32, (PAD, 128), 1)
    weights = jnp.zeros((PAD, 128), F32)
    for c in range(GROUP):
        for e in range(GROUP):
            if e == c:
                continue
            span = jnp.zeros((PAD, 1), F32)
            for m in range(GROUP):
                if m not in (c, e):
                    span = span + one_if((order[m] > order[e]) & (order[m] < order[c])) * totals[m]
            allowed = one_if((order[e] < order[c]) & (end_docs[e] == prev_docs[c]))
            weights = jnp.where(lane == c * GROUP + e, allowed * jnp.exp2(span), weights)
    for d in range(DOCS):
        value = jnp.zeros((PAD, 1), F32)
        for c in range(GROUP):
            ends_here = (ends[d] > order[c] * STRETCH) & (ends[d] <= order[c] * STRETCH + STRETCH)
            value = value + one_if(ends_here & (prev_docs[c] == d)) * jnp.exp2(at_end[c][d])
        weights = jnp.where(lane == GROUP * GROUP + d, value, weights)
    by_row = tn(spread_q, split3(weights))
    for c in range(GROUP):
        state = jnp.zeros((QUARTER, STATE), F32)
        for e in range(GROUP):
            if e != c:
                state = state + by_row[:, c * GROUP + e : c * GROUP + e + 1] * trail[e]
        carried[c] = state
        staged[c] = state.astype(BF16)
    back = [
        remote(4, staged.at[peer], states_in.at[me], peer, r) for r, peer in enumerate(partners)
    ]
    for copy in back:
        copy.start()
    states_in[me] = staged[me]
    for d in range(DOCS):
        state = jnp.zeros((QUARTER, STATE), F32)
        inflow = jnp.zeros((QUARTER, STATE), F32)
        for c in range(GROUP):
            ends_here = one_if(
                (ends[d] > order[c] * STRETCH) & (ends[d] <= order[c] * STRETCH + STRETCH)
            )
            state = state + ends_here * ends_state[c, d]
            inflow = inflow + ends_here * carried[c]
        finals[d] = state + by_row[:, GROUP * GROUP + d : GROUP * GROUP + d + 1] * inflow

    finals_copy.start()
    lax.fori_loop(EARLY, HEADS // 2, pair, 0, unroll=2)

    gate_copy.wait()
    doc_lane = doc_of(lanes + mine * STRETCH)
    carry_t = jnp.where(doc_lane == prev_of(mine), jnp.exp2(log_run[me]), 0.0)
    carry_rows = jnp.transpose(split3(carry_t).astype(F32)).astype(BF16)
    square = jnp.zeros((STRETCH, 128), F32)
    for slot in (me,) + (partners[1], partners[2], partners[0]):
        if slot is not me:
            arrived(4, states_in, slot)

        def read_chunk(c, square):
            cols = pl.ds(pl.multiple_of(slot * QUARTER + c * 128, 128), 128)
            rows = pl.ds(pl.multiple_of(c * 128, 128), 128)
            readout = nt(mixed[:, INNER + STATE :], states_in[slot, rows, :])
            carry = jnp.dot(carry_rows, expand[:, cols], preferred_element_type=F32)
            gated = (y[:, cols] + readout * carry) * silu(gate[:, cols].astype(F32))
            y[:, cols] = gated
            return square + gated * gated

        square = lax.fori_loop(0, QUARTER // 128, read_chunk, square)
    mean = jnp.sum(square, axis=1, keepdims=True) * (1.0 / INNER)
    factor = jnp.broadcast_to(lax.rsqrt(mean + 1e-05), (STRETCH, 128))

    def norm_chunk(c, carry):
        cols = pl.ds(pl.multiple_of(c * 128, 128), 128)
        out[:, cols] = (y[:, cols] * factor * params[5:6, cols]).astype(BF16)
        return carry

    lax.fori_loop(0, INNER // 128, norm_chunk, 0, unroll=2)
    finals_copy.wait()
    for copy in sends + back:
        copy.wait_send()


def fused(
    mixer_in,
    gate_input,
    step_raw,
    lengths,
    deal_order,
    conv_weight,
    conv_bias,
    step_bias,
    decay_rate,
    skip_gain,
    norm_gain,
):
    smem = pl.BlockSpec(memory_space=pltpu.SMEM)
    vmem = pl.BlockSpec(memory_space=pltpu.VMEM)
    anywhere = pl.BlockSpec(memory_space=pl.ANY)
    return pl.pallas_call(
        kernel,
        out_shape=(
            jax.ShapeDtypeStruct((STRETCH, INNER), BF16),
            jax.ShapeDtypeStruct((DOCS, QUARTER, STATE), F32),
        ),
        in_specs=[smem, smem, vmem, anywhere] + [vmem] * 7,
        out_specs=(vmem, anywhere),
        scratch_shapes=[
            pltpu.VMEM((GROUP, PAD, STRETCH), BF16),
            pltpu.VMEM((GROUP, 16, QUARTER), BF16),
            pltpu.VMEM((GROUP, STRETCH, STATE), BF16),
            pltpu.VMEM((GROUP, STRETCH, QUARTER), BF16),
            pltpu.VMEM((GROUP, QUARTER, STATE), BF16),
            pltpu.VMEM((GROUP, QUARTER, STATE), BF16),
            pltpu.VMEM((GROUP, 16, QUARTER), F32),
            pltpu.VMEM((GROUP, 16, QUARTER), F32),
            pltpu.VMEM((STRETCH + 8, CHANNELS), F32),
            pltpu.VMEM((STRETCH, CHANNELS), BF16),
            pltpu.VMEM((STRETCH, STRETCH), F32),
            pltpu.VMEM((STRETCH, INNER), F32),
            pltpu.VMEM((STRETCH + 8, SLOT), F32),
            pltpu.VMEM((STRETCH, QUARTER), BF16),
            pltpu.VMEM((GROUP, DOCS, QUARTER, STATE), F32),
            pltpu.VMEM((GROUP, QUARTER, STATE), F32),
            pltpu.VMEM((GROUP, QUARTER, STATE), F32),
            pltpu.VMEM((GROUP, PAD, STRETCH), F32),
            pltpu.VMEM((GROUP, PAD, STRETCH), F32),
            pltpu.VMEM((GROUP, PAD, STRETCH), F32),
            pltpu.VMEM((ROWS3, STRETCH), BF16),
            pltpu.VMEM((ROWS3, INNER), BF16),
            pltpu.VMEM((KERNEL - 1, STRETCH, 128), F32),
            pltpu.VMEM((8, CHANNELS), F32),
            pltpu.VMEM((8, 128), F32),
            pltpu.VMEM((STRETCH, INNER), BF16),
            pltpu.VMEM((DOCS, QUARTER, STATE), F32),
            pltpu.SemaphoreType.DMA((2,)),
            pltpu.SemaphoreType.DMA((5, GROUP)),
            pltpu.SemaphoreType.DMA((5, GROUP)),
        ],
        compiler_params=pltpu.CompilerParams(
            collective_id=0, has_side_effects=True, vmem_limit_bytes=56 * 1024 * 1024
        ),
    )(
        deal_order,
        lengths,
        mixer_in,
        gate_input,
        step_raw.T,
        conv_weight,
        conv_bias,
        step_bias[None, :],
        decay_rate[None, :],
        skip_gain[None, :],
        norm_gain,
    )


def solution(mesh):
    return jax.shard_map(
        fused if mesh.shape["seq"] == GROUP else body,
        mesh=mesh,
        in_specs=(
            P(("dp", "seq"), None),
            P(("dp", "seq"), None),
            P(("dp", "seq"), None),
            P("dp"),
            P("dp"),
            P(),
            P(),
            P(),
            P(),
            P(),
            P(),
        ),
        out_specs=(P(("dp", "seq"), None), P("dp", "seq", None)),
        check_vma=False,
    )
```
